32 devices in a mesh: grp: 2 (over y), row: 4 (over z), col: 2 (over x), dep: 2 (over core).
Axes of the slice: x: 2, y: 2, z: 4, core: 2. Of those that a mesh axis runs over, the one named last changes fastest.
Arguments:
- alignment_embedding: bfloat16 [512, 64, 64], P(('grp', 'dep'), ('row', 'col')), parts along dimension 0, may hold values from -6 to 6
- contact_embedding: float32 [128, 64, 128], P(('grp', 'row', 'dep'), 'col'), parts along dimension 0, may hold values from -6 to 6
- alignment_feedforward_multiplier: float32 [2, 64], replicated, may hold values from 0.25 to 1.75
- alignment_expand_matrix: bfloat16 [2, 2, 64, 256], replicated, may hold values from -0.75 to 0.75
- alignment_contract_matrix: bfloat16 [2, 256, 64], replicated, may hold values from -0.375 to 0.375
- product_standardize_multiplier: float32 [2, 64], replicated, may hold values from 0.25 to 1.75
- first_operand_matrix: bfloat16 [2, 64, 32], replicated, may hold values from -0.75 to 0.75
- second_operand_matrix: bfloat16 [2, 64, 32], replicated, may hold values from -0.75 to 0.75
- product_result_matrix: bfloat16 [2, 1024, 128], replicated, may hold values from -2 to 2
- product_result_offset: float32 [2, 128], replicated, may hold values from -3 to 3
- contact_feedforward_multiplier: float32 [2, 128], replicated, may hold values from 0.25 to 1.75
- contact_expand_matrix: bfloat16 [2, 2, 128, 512], replicated, may hold values from -0.5 to 0.5
- contact_contract_matrix: bfloat16 [2, 512, 128], replicated, may hold values from -0.25 to 0.25
Outputs:
- pair_out: float32 [128, 64, 128], P(('grp', 'row', 'dep'), 'col'), parts along dimension 0
The draws below stay inside these ranges and needn't reach their ends.
There are 2 independent parts, one for each index of `grp`. The reference program is written for one: setup_inputs(seed, part) draws one part's arguments, and reference() takes and returns one part's arrays. A program takes and returns all parts, laid end to end along the dimension named above; an argument that names none is the same for every part. Nothing has to cross between parts.
All inputs are finite; a program needn't handle non-finite values.
Results may differ from the reference program's by a relative error of at most 0.0062.
Values may be sent and summed in bfloat16 or wider, within the bound.
No kernel may reach another device: no remote copies, remote signals or barrier semaphores. Data moves between devices by JAX's collectives and lax.ppermute only.
A program may use at most 128 MiB of HBM per device.

```python
import jax
import jax.numpy as jnp
from jax import lax

ALIGN_FEATURES = 64
PROJ_DEPTH = 32
PC = 128
TRANS = 512
ALIGN_EXPANSION = 256
NUM_MODULES = 2
S_HALF = 128
NUM_ALIGNED = 256
NUM_AMINO = 64
N_ROW = 4


def level_of(rng, dims, split, least, top_value):
    level = 1.0
    for dim, shards_of in split:
        steps = jax.random.uniform(jax.random.fold_in(jax.random.fold_in(rng, 6), dim), (shards_of,), jnp.float32, least / len(split), top_value / len(split))
        level = level * jnp.repeat(jnp.exp(steps), dims[dim] // shards_of).reshape((-1,) + (1,) * (len(dims) - 1 - dim))
    return level


def bell_draw(rng, dims, scale, most, split=(), kind=jnp.bfloat16):
    drawn = jax.random.normal(rng, dims, jnp.float32) * scale
    if len(split) > 0:
        drawn = level_of(rng, dims, split, -0.22, 0.18) * drawn
    return jnp.clip(drawn, min=-most, max=most).astype(kind)


def setup_inputs(seed: int = 0, part: int = 0) -> dict:
    key_list = jax.random.split(jax.random.key(seed), 14)
    part_splits = jax.random.split(jax.random.fold_in(key_list[13], part), 14)
    return {
        "alignment_embedding": bell_draw(part_splits[0], (NUM_ALIGNED, NUM_AMINO, ALIGN_FEATURES), 1.0, 6.0, ((0, 2), (1, 8))),
        "contact_embedding": bell_draw(part_splits[1], (NUM_AMINO, NUM_AMINO, PC), 1.0, 6.0, ((0, 8), (1, 2)), jnp.float32),
        "alignment_feedforward_multiplier": jnp.clip(1.0 + 0.15 * jax.random.normal(key_list[2], (NUM_MODULES, ALIGN_FEATURES), jnp.float32), 0.25, 1.75),
        "alignment_expand_matrix": bell_draw(key_list[3], (NUM_MODULES, 2, ALIGN_FEATURES, ALIGN_EXPANSION), ALIGN_FEATURES ** -0.5, 0.75),
        "alignment_contract_matrix": bell_draw(key_list[4], (NUM_MODULES, ALIGN_EXPANSION, ALIGN_FEATURES), ALIGN_EXPANSION ** -0.5, 0.375),
        "product_standardize_multiplier": jnp.clip(1.0 + 0.15 * jax.random.normal(key_list[5], (NUM_MODULES, ALIGN_FEATURES), jnp.float32), 0.25, 1.75),
        "first_operand_matrix": bell_draw(key_list[6], (NUM_MODULES, ALIGN_FEATURES, PROJ_DEPTH), ALIGN_FEATURES ** -0.5, 0.75),
        "second_operand_matrix": bell_draw(key_list[7], (NUM_MODULES, ALIGN_FEATURES, PROJ_DEPTH), ALIGN_FEATURES ** -0.5, 0.75),
        "product_result_matrix": bell_draw(key_list[8], (NUM_MODULES, PROJ_DEPTH * PROJ_DEPTH, PC), (PROJ_DEPTH * PROJ_DEPTH // S_HALF) ** -0.5, 2.0),
        "product_result_offset": bell_draw(key_list[9], (NUM_MODULES, PC), 0.5, 3.0, (), jnp.float32),
        "contact_feedforward_multiplier": jnp.clip(1.0 + 0.15 * jax.random.normal(key_list[10], (NUM_MODULES, PC), jnp.float32), 0.25, 1.75),
        "contact_expand_matrix": bell_draw(key_list[11], (NUM_MODULES, 2, PC, TRANS), PC ** -0.5, 0.5),
        "contact_contract_matrix": bell_draw(key_list[12], (NUM_MODULES, TRANS, PC), TRANS ** -0.5, 0.25),
    }


def standardize_features(values, gain):
    mean = lax.optimization_barrier(jnp.mean(values, axis=-1, keepdims=True))
    centered = values - mean
    var = lax.optimization_barrier(jnp.mean(centered * centered, axis=-1, keepdims=True))
    return centered * lax.rsqrt(var + 1e-05) * gain

def swish_gating(inputs, w_in, w_out):
    gate = jnp.dot(inputs, w_in[0], preferred_element_type=jnp.float32)
    upper = jnp.dot(inputs, w_in[1], preferred_element_type=jnp.float32)
    hidden = (jax.nn.silu(gate) * upper).astype(jnp.bfloat16)
    return jnp.dot(hidden, w_out, preferred_element_type=jnp.float32)

def reference(alignment_embedding, contact_embedding, alignment_feedforward_multiplier, alignment_expand_matrix, alignment_contract_matrix, product_standardize_multiplier, first_operand_matrix, second_operand_matrix, product_result_matrix, product_result_offset, contact_feedforward_multiplier, contact_expand_matrix, contact_contract_matrix):
    projection_depth, amino_total, feature_total = alignment_embedding.shape
    width = first_operand_matrix.shape[2]
    pair_ch = contact_embedding.shape[2]
    block_rows = amino_total // N_ROW
    module_carry = alignment_embedding.astype(jnp.float32)
    field = contact_embedding
    for module_step in range(NUM_MODULES):
        standardized_source = standardize_features(module_carry, alignment_feedforward_multiplier[module_step]).astype(jnp.bfloat16).reshape(-1, feature_total)
        module_carry = module_carry + swish_gating(standardized_source, alignment_expand_matrix[module_step], alignment_contract_matrix[module_step]).reshape(module_carry.shape)
        standardized_source = standardize_features(module_carry, product_standardize_multiplier[module_step]).astype(jnp.bfloat16).reshape(-1, feature_total)
        left = jnp.dot(standardized_source, first_operand_matrix[module_step], preferred_element_type=jnp.float32).astype(jnp.bfloat16).reshape(projection_depth, amino_total, width)
        right = jnp.dot(standardized_source, second_operand_matrix[module_step], preferred_element_type=jnp.float32).astype(jnp.bfloat16).reshape(projection_depth, amino_total * width)
        w_out = product_result_matrix[module_step].astype(jnp.float32)

        def block(start):
            left_blk = lax.dynamic_slice_in_dim(left, start, block_rows, 1).reshape(projection_depth, block_rows * width)
            outer = lax.dot_general(left_blk, right, (((0,), (0,)), ((), ())), preferred_element_type=jnp.float32)
            outer = outer.reshape(block_rows, width, amino_total, width).transpose(0, 2, 1, 3).reshape(block_rows * amino_total, width * width) / projection_depth
            return jnp.dot(outer, w_out, precision=lax.Precision.HIGHEST).reshape(block_rows, amino_total, pair_ch)
        starts = jnp.arange(N_ROW, dtype=jnp.int32) * block_rows
        projected = lax.map(block, starts).reshape(amino_total, amino_total, pair_ch)
        field = field + projected + product_result_offset[module_step]
        standardized_source = standardize_features(field, contact_feedforward_multiplier[module_step]).astype(jnp.bfloat16).reshape(-1, pair_ch)
        field = field + swish_gating(standardized_source, contact_expand_matrix[module_step], contact_contract_matrix[module_step]).reshape(field.shape)
    return field
```

```python
import functools

import jax
import jax.numpy as jnp
from jax import lax
from jax.experimental import pallas as pl
from jax.experimental.pallas import tpu as pltpu
from jax.sharding import PartitionSpec as P

NUM_MODULES = 2
LANES = 128
SUB = 8
F32 = jnp.float32
BF16 = jnp.bfloat16
VMEM_LIMIT = 32 * 1024 * 1024


def dot_tn(a, b):
    return lax.dot_general(a, b, (((0,), (0,)), ((), ())), preferred_element_type=F32)


def dot_nt(a, b):
    return lax.dot_general(a, b, (((1,), (1,)), ((), ())), preferred_element_type=F32)


def dot_nn(a, b):
    return lax.dot_general(a, b, (((1,), (0,)), ((), ())), preferred_element_type=F32)


def silu(x):
    return x * (1.0 / (1.0 + jnp.exp(-x)))


def norm_rows(m, gain):
    mean = jnp.mean(m, axis=0, keepdims=True)
    centered = m - mean
    var = jnp.mean(centered * centered, axis=0, keepdims=True)
    return centered * lax.rsqrt(var + 1e-05) * gain


def norm_lanes(x, gain):
    mean = jnp.mean(x, axis=1, keepdims=True)
    centered = x - mean
    var = jnp.mean(centered * centered, axis=1, keepdims=True)
    return centered * lax.rsqrt(var + 1e-05) * gain


def column_gain(g_ref, step, lanes):
    row = g_ref[step : step + 1, :]
    return jnp.broadcast_to(row, (lanes, row.shape[1])).T


def msa_kernel(step, first, seqs, amino, m_ref, g1_ref, win_ref, wout_ref, g2_ref, wl_ref, wr_ref, *rest):
    if first:
        m_out, left_out, right_out, xs, ls = rest
        xs[...] = m_ref[...].astype(F32)
    else:
        left_out, right_out, ls = rest
    width = wl_ref.shape[2]
    per = 2
    lanes = per * seqs
    gain1 = column_gain(g1_ref, step, lanes)
    gain2 = column_gain(g2_ref, step, lanes)
    for start in range(0, amino, per):
        if first:
            m = jnp.concatenate(
                [xs[pl.ds(start + k, seqs, stride=amino), :].T for k in range(per)], axis=1
            )
        else:
            m = m_ref[:, start * seqs : start * seqs + lanes]
        xm = norm_rows(m, gain1).astype(BF16)
        gate = dot_tn(win_ref[step, 0], xm)
        upper = dot_tn(win_ref[step, 1], xm)
        hidden = (silu(gate) * upper).astype(BF16)
        m = m + dot_tn(wout_ref[step], hidden)
        if first:
            m_out[:, start * seqs : start * seqs + lanes] = m
        xo = norm_rows(m, gain2).astype(BF16)
        left = dot_tn(wl_ref[step], xo)
        right = dot_tn(wr_ref[step], xo)
        for k in range(per):
            rows = slice((start + k) * width, (start + k + 1) * width)
            ls[rows, :] = left[:, k * seqs : (k + 1) * seqs]
            right_out[rows, :] = right[:, k * seqs : (k + 1) * seqs].astype(BF16)
    for p in range(0, width, 2):
        pair = [ls[pl.ds(p + k, amino, stride=width), :] for k in range(2)]
        left_out[p * amino : (p + 2) * amino, :] = jnp.concatenate(pair, axis=0).astype(BF16)


def msa_call(step, first, seqs, amino, m, g1, win, wout, g2, wl, wr):
    width = wl.shape[2]
    feats = win.shape[2]
    factor = jax.ShapeDtypeStruct((amino * width, seqs), BF16)
    outs = [factor, factor]
    scratch = [pltpu.VMEM((amino * width, seqs), F32)]
    if first:
        outs = [jax.ShapeDtypeStruct((feats, amino * seqs), F32)] + outs
        scratch = [pltpu.VMEM((seqs * amino, feats), F32)] + scratch
    return pl.pallas_call(
        functools.partial(msa_kernel, step, first, seqs, amino),
        out_shape=outs,
        in_specs=[pl.BlockSpec(memory_space=pltpu.VMEM)] * 7,
        out_specs=[pl.BlockSpec(memory_space=pltpu.VMEM)] * len(outs),
        scratch_shapes=scratch,
        compiler_params=pltpu.CompilerParams(vmem_limit_bytes=VMEM_LIMIT),
        cost_estimate=pl.CostEstimate(flops=150_000_000, bytes_accessed=500_000, transcendentals=300_000),
        name="msa" + str(step),
    )(m, g1, win, wout, g2, wl, wr)


def swap_groups(parts, width):
    n = len(parts)
    lanes = parts[0].shape[1]
    group = lax.broadcasted_iota(jnp.int32, parts[0].shape, 1) // width
    bit = 1
    while bit < n:
        low = (group & bit) == 0
        shift = bit * width
        new = list(parts)
        for a in range(n):
            if a & bit == 0:
                x, y = parts[a], parts[a | bit]
                new[a] = jnp.where(low, x, pltpu.roll(y, shift, 1))
                new[a | bit] = jnp.where(low, pltpu.roll(x, lanes - shift, 1), y)
        parts = new
        bit *= 2
    return parts


def pair_kernel(step, n_row, n_col, n_dep, amino, width, depth, *refs):
    lefts, rest = refs[:n_col], refs[n_col:]
    rights, (w_ref, keep_ref, send_ref, ls, rs, g_scr, a_scr) = rest[:n_row], rest[n_row:]
    ratio = n_row // n_col
    per_dep = n_col // n_dep
    row, col, dep = lax.axis_index("row"), lax.axis_index("col"), lax.axis_index("dep")
    for dc in range(n_col):
        source = lax.rem(col - dc + n_col, n_col)
        slot = lax.rem(source - dep * per_dep + n_col, n_col)
        ls[slot] = lefts[dc][...]
    for dr in range(ratio):
        off = lax.rem(lax.rem(row, ratio) - dr + ratio, ratio)
        for dc in range(n_col):
            source = lax.rem(col - dc + n_col, n_col)
            rs[off * n_col + source] = rights[dr * n_col + dc][...]
    block = rs.shape[1]
    right = rs[...].reshape(n_row * block, rs.shape[2])
    groups = LANES // width
    tiles = n_row * block // LANES
    rows_tile = groups * amino

    def relayout(t):
        lane = pl.ds(t * LANES, LANES) if isinstance(t, int) else pl.ds(pl.multiple_of(t * LANES, LANES), LANES)
        for big in range(width // groups):
            parts = [
                g_scr[(big * groups + k) * amino : (big * groups + k + 1) * amino, lane] for k in range(groups)
            ]
            parts = swap_groups(parts, width)
            a_scr[pl.ds(t * rows_tile, rows_tile), big * LANES : (big + 1) * LANES] = jnp.concatenate(
                parts, axis=0
            ).astype(BF16)

    def one_left(blk):
        g_scr[...] = dot_nt(ls[blk], right)
        if tiles <= 8:
            for t in range(tiles):
                relayout(t)
        else:
            lax.fori_loop(0, tiles, lambda t, _: (relayout(t), 0)[1], 0)
        return dot_nn(a_scr[...], w_ref[step]) * (1.0 / depth)

    for blk in range(per_dep):
        keep_ref[blk] = one_left(blk)
    for blk in range(per_dep, n_col):
        send_ref[blk - per_dep] = one_left(blk)


def pair_call(step, n_row, n_col, n_dep, amino, width, depth, lefts, rights, w):
    rows = n_row * amino * amino
    pair_ch = w.shape[2]
    per_dep = n_col // n_dep
    out = jax.ShapeDtypeStruct((per_dep, rows, pair_ch), F32)
    send = jax.ShapeDtypeStruct((n_col - per_dep, rows, pair_ch), F32)
    block, seqs = rights[0].shape
    return pl.pallas_call(
        functools.partial(pair_kernel, step, n_row, n_col, n_dep, amino, width, depth),
        out_shape=[out, send],
        in_specs=[pl.BlockSpec(memory_space=pltpu.VMEM)] * (n_col + n_row + 1),
        out_specs=[pl.BlockSpec(memory_space=pltpu.VMEM)] * 2,
        scratch_shapes=[
            pltpu.VMEM((n_col, block, seqs), BF16),
            pltpu.VMEM((n_row, block, seqs), BF16),
            pltpu.VMEM((block, n_row * block), F32),
            pltpu.VMEM((rows, width * width), BF16),
        ],
        compiler_params=pltpu.CompilerParams(vmem_limit_bytes=VMEM_LIMIT),
        cost_estimate=pl.CostEstimate(flops=600_000_000, bytes_accessed=1_500_000, transcendentals=0),
        name="pair" + str(step),
    )(*lefts, *rights, w)


def trans_kernel(step, first, last, amino, cols, z_ref, keep_ref, recv_ref, b_ref, g_ref, win_ref, wout_ref, out_ref):
    for blk in range(keep_ref.shape[0]):
        base = blk * amino * cols
        if first:
            z = jnp.concatenate([z_ref[pl.ds(base + j, amino, stride=cols), :] for j in range(cols)], axis=0)
        else:
            z = z_ref[blk]
        z = z + (keep_ref[blk] + recv_ref[blk]) + b_ref[step : step + 1, :]
        xp = norm_lanes(z, g_ref[step : step + 1, :]).astype(BF16)
        gate = dot_nn(xp, win_ref[step, 0])
        upper = dot_nn(xp, win_ref[step, 1])
        hidden = (silu(gate) * upper).astype(BF16)
        z = z + dot_nn(hidden, wout_ref[step])
        if last:
            for j in range(cols):
                out_ref[pl.ds(base + j, amino, stride=cols), :] = z[j * amino : (j + 1) * amino, :]
        else:
            out_ref[blk] = z


def trans_call(step, amino, cols, z, keep, recv, b, g, win, wout):
    first, last = step == 0, step == NUM_MODULES - 1
    per_dep, rows, pair_ch = keep.shape
    shape = (per_dep * rows, pair_ch) if last else keep.shape
    return pl.pallas_call(
        functools.partial(trans_kernel, step, first, last, amino, cols),
        out_shape=jax.ShapeDtypeStruct(shape, F32),
        in_specs=[pl.BlockSpec(memory_space=pltpu.VMEM)] * 7,
        out_specs=pl.BlockSpec(memory_space=pltpu.VMEM),
        compiler_params=pltpu.CompilerParams(vmem_limit_bytes=VMEM_LIMIT),
        cost_estimate=pl.CostEstimate(flops=150_000_000, bytes_accessed=1_500_000, transcendentals=300_000),
        name="trans" + str(step),
    )(z, keep, recv, b, g, win, wout)


def per_device(n_row, n_col, n_dep, msa, pair, g_ff, w_in, w_out, g_op, w_l, w_r, w_res, b_res, g_pair, p_in, p_out):
    seqs, amino, feats = msa.shape
    width = w_l.shape[2]
    depth = seqs * n_dep
    ratio = n_row // n_col
    cols = amino * n_row
    row, col = lax.axis_index("row"), lax.axis_index("col")

    def rows_by(k):
        return lambda x: lax.ppermute(x, "row", [(r, (r + k) % n_row) for r in range(n_row)])

    def group_by(k):
        pairs = [(r, r // ratio * ratio + (r % ratio + k) % ratio) for r in range(n_row)]
        return lambda x: lax.ppermute(x, "row", pairs)

    def cols_by(k):
        return lambda x: lax.ppermute(x, "col", [(c, (c + k) % n_col) for c in range(n_col)])

    def pick(items, index):
        got = items[0]
        for k in range(1, len(items)):
            got = jnp.where(index == k, items[k], got)
        return got

    def spread_far(right):
        return [right] + [rows_by(k * ratio)(right) for k in range(1, n_col)]

    def spread_cols(items):
        group = row // ratio
        wanted = [pick(items, (group - (col + dc) + 2 * n_col) % n_col) for dc in range(n_col)]
        return [wanted[0]] + [cols_by(dc)(wanted[dc]) for dc in range(1, n_col)]

    def spread_rows(items):
        both = jnp.concatenate(items, axis=0)
        size = items[0].shape[0]
        got = list(items)
        for dr in range(1, ratio):
            moved = group_by(dr)(both)
            got += [moved[k * size : (k + 1) * size] for k in range(n_col)]
        return got

    m, left0, right0 = msa_call(
        0, True, seqs, amino, msa.reshape(seqs * amino, feats), g_ff, w_in, w_out, g_op, w_l, w_r
    )
    left1, right1 = msa_call(1, False, seqs, amino, m, g_ff, w_in, w_out, g_op, w_l, w_r)
    z = pair.reshape(-1, pair.shape[2])
    far = [spread_far(right0), spread_far(right1)]
    lefts = [
        [left] + [cols_by(dc)(left) for dc in range(1, n_col)] for left in (left0, left1)
    ]
    for step in range(NUM_MODULES):
        rights = spread_rows(spread_cols(far[step]))
        keep, send = pair_call(
            step, n_row, n_col, n_dep, amino, width, depth, lefts[step], rights, w_res
        )
        recv = lax.ppermute(send, "dep", [(d, (d + 1) % n_dep) for d in range(n_dep)])
        z = trans_call(step, amino, cols, z, keep, recv, b_res, g_pair, p_in, p_out)
    return z.reshape(pair.shape)


def solution(mesh):
    return jax.shard_map(
        functools.partial(per_device, mesh.shape["row"], mesh.shape["col"], mesh.shape["dep"]),
        mesh=mesh,
        in_specs=(
            P(("grp", "dep"), ("row", "col"), None),
            P(("grp", "row", "dep"), "col", None),
        )
        + (P(),) * 11,
        out_specs=P(("grp", "row", "dep"), "col", None),
        check_vma=False,
    )
```

```python
import functools

import jax
import jax.numpy as jnp
from jax import lax
from jax.experimental import pallas as pl
from jax.experimental.pallas import tpu as pltpu
from jax.sharding import PartitionSpec as P

NUM_MODULES = 2
LANES = 128
SUB = 8
F32 = jnp.float32
BF16 = jnp.bfloat16
VMEM_LIMIT = 32 * 1024 * 1024


def dot_tn(a, b):
    return lax.dot_general(a, b, (((0,), (0,)), ((), ())), preferred_element_type=F32)


def dot_nt(a, b):
    return lax.dot_general(a, b, (((1,), (1,)), ((), ())), preferred_element_type=F32)


def dot_nn(a, b):
    return lax.dot_general(a, b, (((1,), (0,)), ((), ())), preferred_element_type=F32)


def silu_of_double(x):
    return x * jnp.tanh(x) + x


def norm_rows(m, gain):
    mean = jnp.mean(m, axis=0, keepdims=True)
    centered = m - mean
    var = jnp.mean(centered * centered, axis=0, keepdims=True)
    return centered * lax.rsqrt(var + 1e-05) * gain


def norm_lanes(x, gain):
    mean = jnp.mean(x, axis=1, keepdims=True)
    centered = x - mean
    var = jnp.mean(centered * centered, axis=1, keepdims=True)
    return centered * lax.rsqrt(var + 1e-05) * gain


def msa_module(step, seqs, amino, m_ref, gains, w_in, w_out, w_l, w_r, m_out, left_out, right_out, ls):
    width = w_r.shape[1]
    per = 8
    lanes = per * seqs
    three = len(m_ref.shape) == 3
    gain1 = jnp.concatenate([gains[step, 0]] * per, axis=1)
    gain2 = jnp.concatenate([gains[step, 1]] * per, axis=1)
    for start in range(0, amino, per):
        here = slice(start * seqs, start * seqs + lanes)
        if three:
            m = jnp.concatenate([m_ref[start + k] for k in range(per)], axis=1).astype(F32)
        else:
            m = m_ref[:, here]
        xm = norm_rows(m, gain1).astype(BF16)
        gate = dot_nn(w_in[step, 0], xm)
        upper = dot_nn(w_in[step, 1], xm)
        hidden = (silu_of_double(gate) * upper).astype(BF16)
        m = m + dot_nn(w_out[step], hidden)
        if m_out is not None:
            m_out[:, here] = m
        xo = norm_rows(m, gain2).astype(BF16)
        right = dot_nn(w_r[step], xo)
        if left_out is not None:
            left = dot_nn(w_l[step], xo)
        for k in range(per):
            rows = slice((start + k) * width, (start + k + 1) * width)
            right_out[rows, :] = right[:, k * seqs : (k + 1) * seqs].astype(BF16)
            if left_out is not None:
                ls[rows, :] = left[:, k * seqs : (k + 1) * seqs]
    if left_out is not None:
        for p in range(0, width, 2):
            pair = [ls[pl.ds(p + k, amino, stride=width), :] for k in range(2)]
            left_out[p * amino : (p + 2) * amino, :] = jnp.concatenate(pair, axis=0).astype(BF16)


def own_kernel(seqs, amino, n_first, n_load, *refs):
    srcs, refs = refs[:n_load], refs[n_load:]
    (lefts_out, rights_out, gains, w_in), refs = refs[:4], refs[4:]
    dsts, (m_ref, g1_ref, win_ref, g2_ref, state, ls, sems) = refs[: n_load - 4], refs[n_load - 4 :]
    dsts = (m_ref, g1_ref, win_ref, g2_ref) + tuple(dsts)
    copies = [pltpu.make_async_copy(s, d, sems.at[k]) for k, (s, d) in enumerate(zip(srcs, dsts))]
    for copy in copies:
        copy.start()
    for copy in copies[:n_first]:
        copy.wait()
    w_out, w_l, w_r = dsts[4:7]
    for step in range(NUM_MODULES):
        for k, g_ref in enumerate((g1_ref, g2_ref)):
            row = g_ref[step : step + 1, :]
            gains[step, k] = jnp.broadcast_to(row, (seqs, row.shape[1])).T
        for k in range(2):
            w_in[step, k] = win_ref[step, k].T * (1.0 if k else 0.5)
    for step in range(NUM_MODULES):
        source = state if step else m_ref
        target = None if step == NUM_MODULES - 1 else state
        msa_module(
            step, seqs, amino, source, gains, w_in, w_out, w_l, w_r, target, lefts_out.at[step], rights_out.at[step], ls
        )
    for copy in copies[n_first:]:
        copy.wait()


def own_call(seqs, amino, load, n_first):
    m, g1, win, g2, w_out, w_l, w_r = load[:7]
    width, feats, hidden = w_l.shape[1], win.shape[2], win.shape[3]
    factor = jax.ShapeDtypeStruct((NUM_MODULES, amino * width, seqs), BF16)
    outs = [
        factor,
        factor,
        jax.ShapeDtypeStruct((NUM_MODULES, 2, feats, seqs), F32),
        jax.ShapeDtypeStruct((NUM_MODULES, 2, hidden, feats), BF16),
    ]
    outs += [jax.ShapeDtypeStruct(x.shape, x.dtype) for x in load[4:]]
    load = [pltpu.with_memory_space_constraint(x, pltpu.HBM) for x in load]
    got = pl.pallas_call(
        functools.partial(own_kernel, seqs, amino, n_first, len(load)),
        out_shape=outs,
        in_specs=[pl.BlockSpec(memory_space=pltpu.HBM)] * len(load),
        out_specs=[pl.BlockSpec(memory_space=pltpu.VMEM)] * len(outs),
        scratch_shapes=[pltpu.VMEM(x.shape, x.dtype) for x in load[:4]]
        + [
            pltpu.VMEM((feats, amino * seqs), F32),
            pltpu.VMEM((amino * width, seqs), F32),
            pltpu.SemaphoreType.DMA((len(load),)),
        ],
        compiler_params=pltpu.CompilerParams(vmem_limit_bytes=VMEM_LIMIT),
        cost_estimate=pl.CostEstimate(flops=4_000_000_000, bytes_accessed=500_000, transcendentals=0),
        name="own",
    )(*load)
    return list(got[:4]), list(got[4:])


def far_kernel(seqs, amino, m_ref, gains, w_in, w_out, w_r, right_out, state):
    for step in range(NUM_MODULES):
        source = state if step else m_ref
        target = None if step == NUM_MODULES - 1 else state
        msa_module(
            step, seqs, amino, source, gains, w_in, w_out, None, w_r, target, None, right_out.at[step], None
        )


def far_call(seqs, amino, m, gains, w_in, w_out, w_r):
    return pl.pallas_call(
        functools.partial(far_kernel, seqs, amino),
        out_shape=jax.ShapeDtypeStruct((NUM_MODULES, amino * w_r.shape[1], seqs), BF16),
        in_specs=[pl.BlockSpec(memory_space=pltpu.VMEM)] * 5,
        out_specs=pl.BlockSpec(memory_space=pltpu.VMEM),
        scratch_shapes=[pltpu.VMEM((w_in.shape[3], amino * seqs), F32)],
        compiler_params=pltpu.CompilerParams(vmem_limit_bytes=VMEM_LIMIT),
        cost_estimate=pl.CostEstimate(flops=3_000_000_000, bytes_accessed=500_000, transcendentals=0),
        name="far",
    )(m, gains, w_in, w_out, w_r)


def swap_groups(parts, width):
    n = len(parts)
    lanes = parts[0].shape[1]
    group = lax.broadcasted_iota(jnp.int32, parts[0].shape, 1) // width
    bit = 1
    while bit < n:
        low = (group & bit) == 0
        shift = bit * width
        new = list(parts)
        for a in range(n):
            if a & bit == 0:
                x, y = parts[a], parts[a | bit]
                new[a] = jnp.where(low, x, pltpu.roll(y, shift, 1))
                new[a | bit] = jnp.where(low, pltpu.roll(x, lanes - shift, 1), y)
        parts = new
        bit *= 2
    return parts


def pair_kernel(step, n_row, n_col, n_dep, amino, width, depth, starts, *refs):
    lefts, refs = refs[:n_col], refs[n_col:]
    rights, refs = refs[:n_row], refs[n_row:]
    w_ref, b_ref, keep_ref, send_ref, ls, rs = refs
    ratio = n_row // n_col
    per_dep = n_col // n_dep
    block, seqs = amino * width, rs.shape[1]
    row, col, dep = lax.axis_index("row"), lax.axis_index("col"), lax.axis_index("dep")
    for dc in range(n_col):
        source = lax.rem(col - dc + n_col, n_col)
        slot = lax.rem(source - dep * per_dep + n_col, n_col)
        ls[slot] = lefts[dc][starts[dc], step].astype(F32)
    for dr in range(ratio):
        off = lax.rem(lax.rem(row, ratio) - dr + ratio, ratio)
        for dc in range(n_col):
            source = lax.rem(col - dc + n_col, n_col)
            k = dr * n_col + dc
            rs[pl.ds(pl.multiple_of((off * n_col + source) * block, block), block), :] = rights[k][starts[n_col + k], step]
    pair_ch = w_ref.shape[2]
    groups = LANES // width
    both = 2 * amino
    tiles = n_row * block // LANES
    rows_tile = groups * amino

    def right(t):
        if isinstance(t, int):
            return rs[t * LANES : (t + 1) * LANES, :]
        return rs[pl.ds(pl.multiple_of(t * LANES, LANES), LANES), :]

    def swapped(outer):
        bigs = []
        for big in range(width // groups):
            first = big * groups
            bigs.append(
                swap_groups([outer[(first + k) * both : (first + k + 1) * both] for k in range(groups)], width)
            )
        return jnp.concatenate([jnp.concatenate([x[k] for x in bigs], axis=1) for k in range(groups)], axis=0)

    for u in range(per_dep):
        left = jnp.concatenate(
            [ls[u].reshape(width, amino, seqs), ls[per_dep + u].reshape(width, amino, seqs)], axis=1
        )
        left = left.reshape(width * both, seqs).astype(BF16)

        def multiply(t):
            return dot_nt(left, right(t)).astype(BF16)

        def finish(t, lhs):
            got = (dot_nn(lhs, w_ref[step]) * (1.0 / depth)).reshape(groups, both, pair_ch)
            rows = pl.ds(t * rows_tile, rows_tile)
            keep_ref[u, rows, :] = got[:, :amino].reshape(rows_tile, pair_ch) + b_ref[step : step + 1, :]
            send_ref[u, rows, :] = got[:, amino:].reshape(rows_tile, pair_ch)

        if tiles <= 8:
            outer, lhs = multiply(0), None
            for t in range(tiles + 1):
                after = multiply(t + 1) if t + 1 < tiles else None
                if t >= 1:
                    finish(t - 1, lhs)
                if t < tiles:
                    lhs = swapped(outer)
                outer = after
        else:
            lax.fori_loop(0, tiles, lambda t, _: (finish(t, swapped(multiply(t))), 0)[1], 0)


def pair_call(step, n_row, n_col, n_dep, amino, width, depth, lefts, rights, w, b):
    rows = n_row * amino * amino
    pair_ch = w.shape[2]
    per_dep = n_col // n_dep
    factors, starts = zip(*lefts, *rights)
    seqs = factors[0].shape[-1]
    block = amino * width
    out = jax.ShapeDtypeStruct((per_dep, rows, pair_ch), F32)
    return pl.pallas_call(
        functools.partial(pair_kernel, step, n_row, n_col, n_dep, amino, width, depth, starts),
        out_shape=[out, out],
        in_specs=[pl.BlockSpec(memory_space=pltpu.VMEM)] * (n_col + n_row + 2),
        out_specs=[pl.BlockSpec(memory_space=pltpu.VMEM)] * 2,
        scratch_shapes=[
            pltpu.VMEM((n_col, block, seqs), F32),
            pltpu.VMEM((n_row * block, seqs), BF16),
        ],
        compiler_params=pltpu.CompilerParams(vmem_limit_bytes=VMEM_LIMIT),
        cost_estimate=pl.CostEstimate(flops=1_700_000_000, bytes_accessed=1_500_000, transcendentals=0),
        name="pair" + str(step),
    )(*factors, w, b)


def trans_kernel(step, first, last, amino, cols, z_ref, keep_ref, recv_ref, g_ref, win_ref, wout_ref, out_ref):
    for blk in range(keep_ref.shape[0]):
        base = blk * amino * cols
        if first:
            z = jnp.concatenate([z_ref[pl.ds(base + j, amino, stride=cols), :] for j in range(cols)], axis=0)
        else:
            z = z_ref[blk]
        z = z + (keep_ref[blk] + recv_ref[blk])
        xp = norm_lanes(z, g_ref[step : step + 1, :]).astype(BF16)
        gate = dot_nn(xp, win_ref[step, 0]) * 0.5
        upper = dot_nn(xp, win_ref[step, 1])
        hidden = (silu_of_double(gate) * upper).astype(BF16)
        z = z + dot_nn(hidden, wout_ref[step])
        if last:
            for j in range(cols):
                out_ref[pl.ds(base + j, amino, stride=cols), :] = z[j * amino : (j + 1) * amino, :]
        else:
            out_ref[blk] = z


def trans_call(step, amino, cols, z, keep, recv, g, win, wout):
    first, last = step == 0, step == NUM_MODULES - 1
    per_dep, rows, pair_ch = keep.shape
    shape = (per_dep * rows, pair_ch) if last else keep.shape
    return pl.pallas_call(
        functools.partial(trans_kernel, step, first, last, amino, cols),
        out_shape=jax.ShapeDtypeStruct(shape, F32),
        in_specs=[pl.BlockSpec(memory_space=pltpu.VMEM)] * 6,
        out_specs=pl.BlockSpec(memory_space=pltpu.VMEM),
        compiler_params=pltpu.CompilerParams(vmem_limit_bytes=VMEM_LIMIT),
        cost_estimate=pl.CostEstimate(flops=700_000_000, bytes_accessed=1_500_000, transcendentals=0),
        name="trans" + str(step),
    )(z, keep, recv, g, win, wout)


def per_device(n_row, n_col, n_dep, msa, pair, g_ff, w_in, w_out, g_op, w_l, w_r, w_res, b_res, g_pair, p_in, p_out):
    seqs, amino, feats = msa.shape
    width = w_l.shape[2]
    depth = seqs * n_dep
    ratio = n_row // n_col
    cols = amino * n_row
    row, col = lax.axis_index("row"), lax.axis_index("col")

    def rows_by(k):
        return lambda x: lax.ppermute(x, "row", [(r, (r + k) % n_row) for r in range(n_row)])

    def group_by(k):
        pairs = [(r, r // ratio * ratio + (r % ratio + k) % ratio) for r in range(n_row)]
        return lambda x: lax.ppermute(x, "row", pairs)

    def cols_by(k):
        return lambda x: lax.ppermute(x, "col", [(c, (c + k) % n_col) for c in range(n_col)])

    def pick(items, index):
        got = items[0]
        for k in range(1, len(items)):
            got = jnp.where(index == k, items[k], got)
        return got

    def spread_far(right):
        return [right] + [rows_by(k * ratio)(right) for k in range(1, n_col)]

    def moved(x, dr, dc):
        pairs = []
        for r in range(n_row):
            to = r // ratio * ratio + (r % ratio + dr) % ratio
            pairs += [(r * n_col + c, to * n_col + (c + dc) % n_col) for c in range(n_col)]
        return lax.ppermute(x, ("row", "col"), pairs)

    def spread(items):
        group = row // ratio
        wanted = [pick(items, (group - (col + dc) + 2 * n_col) % n_col) for dc in range(n_col)]
        steps = [(dr, dc) for dr in range(ratio) for dc in range(n_col)]
        got = [moved(wanted[dc], dr, dc) if dr or dc else wanted[0] for dr, dc in steps]
        return [(x[None], 0) for x in got]

    w_out, w_l, w_r = (w.transpose(0, 2, 1) for w in (w_out, w_l, w_r))
    m = msa.transpose(1, 2, 0)
    z = pair.reshape(-1, pair.shape[2])
    far = [rows_by(k * ratio)(m) for k in range(1, n_col)]
    load = [m, g_ff, w_in, g_op, w_out, w_l, w_r, w_res, b_res, g_pair, p_in, p_out, z]
    (left, right, gains, w_in), load = own_call(seqs, amino, load, 7)
    w_out, w_l, w_r, w_res, b_res, g_pair, p_in, p_out, z = load
    lefts = [left] + [cols_by(dc)(left) for dc in range(1, n_col)]
    lefts = [(x[None], 0) for x in lefts]
    rights = spread([right] + [far_call(seqs, amino, x, gains, w_in, w_out, w_r) for x in far])
    for step in range(NUM_MODULES):
        keep, send = pair_call(
            step, n_row, n_col, n_dep, amino, width, depth, lefts, rights, w_res, b_res
        )
        recv = lax.ppermute(send, "dep", [(d, (d + 1) % n_dep) for d in range(n_dep)])
        z = trans_call(step, amino, cols, z, keep, recv, g_pair, p_in, p_out)
    return z.reshape(pair.shape)


def solution(mesh):
    return jax.shard_map(
        functools.partial(per_device, mesh.shape["row"], mesh.shape["col"], mesh.shape["dep"]),
        mesh=mesh,
        in_specs=(
            P(("grp", "dep"), ("row", "col"), None),
            P(("grp", "row", "dep"), "col", None),
        )
        + (P(),) * 11,
        out_specs=P(("grp", "row", "dep"), "col", None),
        check_vma=False,
    )
```

```python
import functools

import jax
import jax.numpy as jnp
from jax import lax
from jax.experimental import pallas as pl
from jax.experimental.pallas import tpu as pltpu
from jax.sharding import PartitionSpec as P

NUM_MODULES = 2
LANES = 128
SUB = 8
F32 = jnp.float32
BF16 = jnp.bfloat16
VMEM_LIMIT = 32 * 1024 * 1024


def dot_tn(a, b):
    return lax.dot_general(a, b, (((0,), (0,)), ((), ())), preferred_element_type=F32)


def dot_nt(a, b):
    return lax.dot_general(a, b, (((1,), (1,)), ((), ())), preferred_element_type=F32)


def dot_nn(a, b):
    return lax.dot_general(a, b, (((1,), (0,)), ((), ())), preferred_element_type=F32)


def silu_of_double(x):
    return x * jnp.tanh(x) + x


def norm_rows(m, gain):
    mean = jnp.mean(m, axis=0, keepdims=True)
    centered = m - mean
    var = jnp.mean(centered * centered, axis=0, keepdims=True)
    return centered * lax.rsqrt(var + 1e-05) * gain


def norm_lanes(x, gain):
    mean = jnp.mean(x, axis=1, keepdims=True)
    centered = x - mean
    var = jnp.mean(centered * centered, axis=1, keepdims=True)
    return centered * lax.rsqrt(var + 1e-05) * gain


def msa_module(step, seqs, amino, m_ref, gains, w_in, w_out, w_l, w_r, m_out, left_out, right_out, ls):
    width = w_r.shape[1]
    per = 8
    lanes = per * seqs
    three = len(m_ref.shape) == 3
    gain1 = jnp.concatenate([gains[step, 0]] * per, axis=1)
    gain2 = jnp.concatenate([gains[step, 1]] * per, axis=1)
    for start in range(0, amino, per):
        here = slice(start * seqs, start * seqs + lanes)
        if three:
            m = jnp.concatenate([m_ref[start + k] for k in range(per)], axis=1).astype(F32)
        else:
            m = m_ref[:, here]
        xm = norm_rows(m, gain1).astype(BF16)
        gate = dot_nn(w_in[step, 0], xm)
        upper = dot_nn(w_in[step, 1], xm)
        hidden = (silu_of_double(gate) * upper).astype(BF16)
        m = m + dot_nn(w_out[step], hidden)
        if m_out is not None:
            m_out[:, here] = m
        xo = norm_rows(m, gain2).astype(BF16)
        right = dot_nn(w_r[step], xo)
        if left_out is not None:
            left = dot_nn(w_l[step], xo)
        for k in range(per):
            rows = slice((start + k) * width, (start + k + 1) * width)
            right_out[rows, :] = right[:, k * seqs : (k + 1) * seqs].astype(BF16)
            if left_out is not None:
                ls[rows, :] = left[:, k * seqs : (k + 1) * seqs]
    if left_out is not None:
        for p in range(0, width, 2):
            pair = [ls[pl.ds(p + k, amino, stride=width), :] for k in range(2)]
            left_out[p * amino : (p + 2) * amino, :] = jnp.concatenate(pair, axis=0).astype(BF16)


def own_kernel(seqs, amino, n_first, n_load, *refs):
    srcs, refs = refs[:n_load], refs[n_load:]
    (lefts_out, rights_out, gains, w_in), refs = refs[:4], refs[4:]
    dsts, (m_ref, g1_ref, win_ref, g2_ref, state, ls, sems) = refs[: n_load - 4], refs[n_load - 4 :]
    dsts = (m_ref, g1_ref, win_ref, g2_ref) + tuple(dsts)
    copies = [pltpu.make_async_copy(s, d, sems.at[k]) for k, (s, d) in enumerate(zip(srcs, dsts))]
    for copy in copies:
        copy.start()
    for copy in copies[:n_first]:
        copy.wait()
    w_out, w_l, w_r = dsts[4:7]
    for step in range(NUM_MODULES):
        for k, g_ref in enumerate((g1_ref, g2_ref)):
            row = g_ref[step : step + 1, :]
            gains[step, k] = jnp.broadcast_to(row, (seqs, row.shape[1])).T
        for k in range(2):
            w_in[step, k] = win_ref[step, k].T * (1.0 if k else 0.5)
    for step in range(NUM_MODULES):
        source = state if step else m_ref
        target = None if step == NUM_MODULES - 1 else state
        msa_module(
            step, seqs, amino, source, gains, w_in, w_out, w_l, w_r, target, lefts_out.at[step], rights_out.at[step], ls
        )
    for copy in copies[n_first:]:
        copy.wait()


def own_call(seqs, amino, load, n_first):
    m, g1, win, g2, w_out, w_l, w_r = load[:7]
    width, feats, hidden = w_l.shape[1], win.shape[2], win.shape[3]
    factor = jax.ShapeDtypeStruct((NUM_MODULES, amino * width, seqs), BF16)
    outs = [
        factor,
        factor,
        jax.ShapeDtypeStruct((NUM_MODULES, 2, feats, seqs), F32),
        jax.ShapeDtypeStruct((NUM_MODULES, 2, hidden, feats), BF16),
    ]
    outs += [jax.ShapeDtypeStruct(x.shape, x.dtype) for x in load[4:]]
    load = [pltpu.with_memory_space_constraint(x, pltpu.HBM) for x in load]
    got = pl.pallas_call(
        functools.partial(own_kernel, seqs, amino, n_first, len(load)),
        out_shape=outs,
        in_specs=[pl.BlockSpec(memory_space=pltpu.HBM)] * len(load),
        out_specs=[pl.BlockSpec(memory_space=pltpu.VMEM)] * len(outs),
        scratch_shapes=[pltpu.VMEM(x.shape, x.dtype) for x in load[:4]]
        + [
            pltpu.VMEM((feats, amino * seqs), F32),
            pltpu.VMEM((amino * width, seqs), F32),
            pltpu.SemaphoreType.DMA((len(load),)),
        ],
        compiler_params=pltpu.CompilerParams(vmem_limit_bytes=VMEM_LIMIT),
        cost_estimate=pl.CostEstimate(flops=4_000_000_000, bytes_accessed=500_000, transcendentals=0),
        name="own",
    )(*load)
    return list(got[:4]), list(got[4:])


def far_kernel(seqs, amino, m_ref, gains, w_in, w_out, w_r, right_out, state):
    for step in range(NUM_MODULES):
        source = state if step else m_ref
        target = None if step == NUM_MODULES - 1 else state
        msa_module(
            step, seqs, amino, source, gains, w_in, w_out, None, w_r, target, None, right_out.at[step], None
        )


def far_call(seqs, amino, m, gains, w_in, w_out, w_r):
    return pl.pallas_call(
        functools.partial(far_kernel, seqs, amino),
        out_shape=jax.ShapeDtypeStruct((NUM_MODULES, amino * w_r.shape[1], seqs), BF16),
        in_specs=[pl.BlockSpec(memory_space=pltpu.VMEM)] * 5,
        out_specs=pl.BlockSpec(memory_space=pltpu.VMEM),
        scratch_shapes=[pltpu.VMEM((w_in.shape[3], amino * seqs), F32)],
        compiler_params=pltpu.CompilerParams(vmem_limit_bytes=VMEM_LIMIT),
        cost_estimate=pl.CostEstimate(flops=3_000_000_000, bytes_accessed=500_000, transcendentals=0),
        name="far",
    )(m, gains, w_in, w_out, w_r)


def swap_groups(parts, width):
    n = len(parts)
    lanes = parts[0].shape[1]
    group = lax.broadcasted_iota(jnp.int32, parts[0].shape, 1) // width
    bit = 1
    while bit < n:
        low = (group & bit) == 0
        shift = bit * width
        new = list(parts)
        for a in range(n):
            if a & bit == 0:
                x, y = parts[a], parts[a | bit]
                new[a] = jnp.where(low, x, pltpu.roll(y, shift, 1))
                new[a | bit] = jnp.where(low, pltpu.roll(x, lanes - shift, 1), y)
        parts = new
        bit *= 2
    return parts


def pair_kernel(n_col, n_dep, amino, width, depth, starts, *refs):
    n_right = len(starts) - n_col
    lefts, refs = refs[:n_col], refs[n_col:]
    rights, refs = refs[:n_right], refs[n_right:]
    w_ref, b_ref, keep_ref, send_ref, ls = refs
    per_dep = n_col // n_dep
    block, seqs = ls.shape[2:]
    pair_ch = w_ref.shape[2]
    groups = LANES // width
    both = 2 * amino
    tiles = block // LANES
    rows_tile = groups * amino
    col, dep = lax.axis_index("col"), lax.axis_index("dep")
    for dc in range(n_col):
        source = lax.rem(col - dc + n_col, n_col)
        slot = lax.rem(source - dep * per_dep + n_col, n_col)
        for step in range(NUM_MODULES):
            ls[slot, step] = lefts[dc][starts[dc], step].astype(F32)

    def rows_of(step, u):
        left = jnp.concatenate(
            [ls[u, step].reshape(width, amino, seqs), ls[per_dep + u, step].reshape(width, amino, seqs)], axis=1
        )
        return left.reshape(width * both, seqs).astype(BF16)

    def swapped(outer):
        bigs = []
        for big in range(width // groups):
            first = big * groups
            bigs.append(
                swap_groups([outer[(first + k) * both : (first + k + 1) * both] for k in range(groups)], width)
            )
        return jnp.concatenate([jnp.concatenate([x[k] for x in bigs], axis=1) for k in range(groups)], axis=0)

    left = {(step, u): rows_of(step, u) for step in range(NUM_MODULES) for u in range(per_dep)}
    items = [
        (step, u, k, t)
        for step in range(NUM_MODULES)
        for u in range(per_dep)
        for k in range(n_right)
        for t in range(tiles)
    ]

    def multiply(step, u, k, t):
        tile = rights[k][starts[n_col + k], step, t * LANES : (t + 1) * LANES, :]
        return dot_nt(left[step, u], tile).astype(BF16)

    def finish(step, u, k, t, lhs):
        got = (dot_nn(lhs, w_ref[step]) * (1.0 / depth)).reshape(groups, both, pair_ch)
        rows = slice(t * rows_tile, (t + 1) * rows_tile)
        keep_ref[step, u, k, rows, :] = got[:, :amino].reshape(rows_tile, pair_ch) + b_ref[step : step + 1, :]
        send_ref[step, u, k, rows, :] = got[:, amino:].reshape(rows_tile, pair_ch)

    outer, lhs = multiply(*items[0]), None
    for n in range(len(items) + 1):
        after = multiply(*items[n + 1]) if n + 1 < len(items) else None
        if n >= 1:
            finish(*items[n - 1], lhs)
        if n < len(items):
            lhs = swapped(outer)
        outer = after


def pair_call(name, n_col, n_dep, amino, width, depth, lefts, rights, w, b):
    pair_ch = w.shape[2]
    per_dep = n_col // n_dep
    factors, starts = zip(*lefts, *rights)
    seqs = factors[0].shape[-1]
    out = jax.ShapeDtypeStruct((NUM_MODULES, per_dep, len(rights), amino * amino, pair_ch), F32)
    return pl.pallas_call(
        functools.partial(pair_kernel, n_col, n_dep, amino, width, depth, starts),
        out_shape=[out, out],
        in_specs=[pl.BlockSpec(memory_space=pltpu.VMEM)] * (len(factors) + 2),
        out_specs=[pl.BlockSpec(memory_space=pltpu.VMEM)] * 2,
        scratch_shapes=[pltpu.VMEM((n_col, NUM_MODULES, amino * width, seqs), F32)],
        compiler_params=pltpu.CompilerParams(vmem_limit_bytes=VMEM_LIMIT),
        cost_estimate=pl.CostEstimate(
            flops=600_000_000 * len(rights), bytes_accessed=1_500_000, transcendentals=0
        ),
        name="pair" + name,
    )(*factors, w, b)


def trans_kernel(last, n_row, n_col, amino, cols, steps, done_steps, *refs):
    n = sum(len(group) for group in steps)
    parts, refs = refs[: 2 * len(steps)], refs[2 * len(steps) :]
    done, refs = refs[: len(done_steps)], refs[len(done_steps) :]
    z_ref, g_ref, win_ref, wout_ref, out_ref = refs
    ratio = n_row // n_col
    row, col = lax.axis_index("row"), lax.axis_index("col")
    per_dep, size = parts[0].shape[1], amino * amino

    def first_column(step):
        off = lax.rem(lax.rem(row, ratio) - step[0] + ratio, ratio)
        return (off * n_col + lax.rem(col - step[1] + n_col, n_col)) * amino

    def places(steps):
        return [
            u * amino * cols + first_column(step) + j
            for u in range(per_dep)
            for step in steps
            for j in range(amino)
        ]

    flat = [step for group in steps for step in group]
    here = places(flat)
    z = jnp.concatenate([z_ref[pl.ds(at, amino, stride=cols), :] for at in here], axis=0)
    for step in range(NUM_MODULES):
        moved = [
            parts[2 * k][step, u, i] + parts[2 * k + 1][step, u, i]
            for u in range(per_dep)
            for k, group in enumerate(steps)
            for i in range(len(group))
        ]
        z = z + jnp.concatenate(moved, axis=0)
        xp = norm_lanes(z, g_ref[step : step + 1, :]).astype(BF16)
        gate = dot_nn(xp, win_ref[step, 0]) * 0.5
        upper = dot_nn(xp, win_ref[step, 1])
        hidden = (silu_of_double(gate) * upper).astype(BF16)
        z = z + dot_nn(hidden, wout_ref[step])
    if last:
        for k, at in enumerate(here):
            out_ref[pl.ds(at, amino, stride=cols), :] = z[k * amino : (k + 1) * amino, :]
        for x, group in zip(done, done_steps):
            for k, at in enumerate(places([step for part in group for step in part])):
                out_ref[pl.ds(at, amino, stride=cols), :] = x[k * amino : (k + 1) * amino, :]
    else:
        out_ref[...] = z


def trans_call(name, last, n_row, n_col, amino, cols, steps, parts, done_steps, done, z, g, win, wout):
    per_dep, pair_ch = parts[0].shape[1], z.shape[1]
    n = sum(len(group) for group in steps)
    shape = z.shape if last else (per_dep * n * amino * amino, pair_ch)
    return pl.pallas_call(
        functools.partial(trans_kernel, last, n_row, n_col, amino, cols, steps, done_steps),
        out_shape=jax.ShapeDtypeStruct(shape, F32),
        in_specs=[pl.BlockSpec(memory_space=pltpu.VMEM)] * (len(parts) + len(done) + 4),
        out_specs=pl.BlockSpec(memory_space=pltpu.VMEM),
        compiler_params=pltpu.CompilerParams(vmem_limit_bytes=VMEM_LIMIT),
        cost_estimate=pl.CostEstimate(flops=1_400_000_000, bytes_accessed=1_500_000, transcendentals=0),
        name="trans" + name,
    )(*parts, *done, z, g, win, wout)


def per_device(n_row, n_col, n_dep, msa, pair, g_ff, w_in, w_out, g_op, w_l, w_r, w_res, b_res, g_pair, p_in, p_out):
    seqs, amino, feats = msa.shape
    width = w_l.shape[2]
    depth = seqs * n_dep
    ratio = n_row // n_col
    cols = amino * n_row
    row, col = lax.axis_index("row"), lax.axis_index("col")

    def rows_by(k):
        return lambda x: lax.ppermute(x, "row", [(r, (r + k) % n_row) for r in range(n_row)])

    def group_by(k):
        pairs = [(r, r // ratio * ratio + (r % ratio + k) % ratio) for r in range(n_row)]
        return lambda x: lax.ppermute(x, "row", pairs)

    def cols_by(k):
        return lambda x: lax.ppermute(x, "col", [(c, (c + k) % n_col) for c in range(n_col)])

    def pick(items, index):
        got = items[0]
        for k in range(1, len(items)):
            got = jnp.where(index == k, items[k], got)
        return got

    def spread_far(right):
        return [right] + [rows_by(k * ratio)(right) for k in range(1, n_col)]

    def moved(x, dr, dc):
        pairs = []
        for r in range(n_row):
            to = r // ratio * ratio + (r % ratio + dr) % ratio
            pairs += [(r * n_col + c, to * n_col + (c + dc) % n_col) for c in range(n_col)]
        return lax.ppermute(x, ("row", "col"), pairs)

    def spread(items):
        group = row // ratio
        wanted = [pick(items, (group - (col + dc) + 2 * n_col) % n_col) for dc in range(n_col)]
        return lambda dr, dc: moved(wanted[dc], dr, dc) if dr or dc else wanted[0]

    w_out, w_l, w_r = (w.transpose(0, 2, 1) for w in (w_out, w_l, w_r))
    m = msa.transpose(1, 2, 0)
    z = pair.reshape(-1, pair.shape[2])
    far = [rows_by(k * ratio)(m) for k in range(1, n_col)]
    load = [m, g_ff, w_in, g_op, w_out, w_l, w_r, w_res, b_res, g_pair, p_in, p_out, z]
    (left, right, gains, w_in), load = own_call(seqs, amino, load, 7)
    w_out, w_l, w_r, w_res, b_res, g_pair, p_in, p_out, z = load
    lefts = [left] + [cols_by(dc)(left) for dc in range(1, n_col)]
    lefts = [(x[None], 0) for x in lefts]
    take = spread([right] + [far_call(seqs, amino, x, gains, w_in, w_out, w_r) for x in far])
    steps = [[(0, dc) for dc in range(n_col)]]
    for dr in range(1, ratio):
        group = [(dr, dc) for dc in range(n_col)]
        steps += [[step] for step in group] if ratio <= 2 else [group]
    got = [[(take(*step)[None], 0) for step in group] for group in steps]
    parts = []
    for k, rights in enumerate(got):
        keep, send = pair_call(str(k), n_col, n_dep, amino, width, depth, lefts, rights, w_res, b_res)
        parts += [keep, lax.ppermute(send, "dep", [(d, (d + 1) % n_dep) for d in range(n_dep)])]
    call = lambda name, last, *args: trans_call(
        name, last, n_row, n_col, amino, cols, *args, z, g_pair, p_in, p_out
    )
    most = call("0", False, steps[:-1], parts[:-2], [], [])
    z = call("1", True, steps[-1:], parts[-2:], [steps[:-1]], [most])
    return z.reshape(pair.shape)


def solution(mesh):
    return jax.shard_map(
        functools.partial(per_device, mesh.shape["row"], mesh.shape["col"], mesh.shape["dep"]),
        mesh=mesh,
        in_specs=(
            P(("grp", "dep"), ("row", "col"), None),
            P(("grp", "row", "dep"), "col", None),
        )
        + (P(),) * 11,
        out_specs=P(("grp", "row", "dep"), "col", None),
        check_vma=False,
    )
```

```python
import functools

import jax
import jax.numpy as jnp
from jax import lax
from jax.experimental import pallas as pl
from jax.experimental.pallas import tpu as pltpu
from jax.sharding import PartitionSpec as P

NUM_MODULES = 2
LANES = 128
SUB = 8
F32 = jnp.float32
BF16 = jnp.bfloat16
VMEM_LIMIT = 32 * 1024 * 1024


def dot_tn(a, b):
    return lax.dot_general(a, b, (((0,), (0,)), ((), ())), preferred_element_type=F32)


def dot_nt(a, b):
    return lax.dot_general(a, b, (((1,), (1,)), ((), ())), preferred_element_type=F32)


def dot_nn(a, b):
    return lax.dot_general(a, b, (((1,), (0,)), ((), ())), preferred_element_type=F32)


def silu_of_double(x):
    return x * jnp.tanh(x) + x


def norm_rows(m, gain):
    mean = jnp.mean(m, axis=0, keepdims=True)
    centered = m - mean
    var = jnp.mean(centered * centered, axis=0, keepdims=True)
    return centered * lax.rsqrt(var + 1e-05) * gain


def norm_lanes(x, gain):
    mean = jnp.mean(x, axis=1, keepdims=True)
    centered = x - mean
    var = jnp.mean(centered * centered, axis=1, keepdims=True)
    return centered * lax.rsqrt(var + 1e-05) * gain


def msa_module(step, seqs, amino, m_ref, gains, w_in, w_out, w_l, w_r, m_out, left_out, right_out, ls):
    width = w_r.shape[1]
    per = 8
    lanes = per * seqs
    three = len(m_ref.shape) == 3
    gain1 = jnp.concatenate([gains[step, 0]] * per, axis=1)
    gain2 = jnp.concatenate([gains[step, 1]] * per, axis=1)
    for start in range(0, amino, per):
        here = slice(start * seqs, start * seqs + lanes)
        if three:
            m = jnp.concatenate([m_ref[start + k] for k in range(per)], axis=1).astype(F32)
        else:
            m = m_ref[:, here]
        xm = norm_rows(m, gain1).astype(BF16)
        gate = dot_nn(w_in[step, 0], xm)
        upper = dot_nn(w_in[step, 1], xm)
        hidden = (silu_of_double(gate) * upper).astype(BF16)
        m = m + dot_nn(w_out[step], hidden)
        if m_out is not None:
            m_out[:, here] = m
        xo = norm_rows(m, gain2).astype(BF16)
        right = dot_nn(w_r[step], xo)
        if left_out is not None:
            left = dot_nn(w_l[step], xo)
        for k in range(per):
            rows = slice((start + k) * width, (start + k + 1) * width)
            right_out[rows, :] = right[:, k * seqs : (k + 1) * seqs].astype(BF16)
            if left_out is not None:
                ls[rows, :] = left[:, k * seqs : (k + 1) * seqs]
    if left_out is not None:
        for p in range(0, width, 2):
            pair = [ls[pl.ds(p + k, amino, stride=width), :] for k in range(2)]
            left_out[p * amino : (p + 2) * amino, :] = jnp.concatenate(pair, axis=0).astype(BF16)


def own_kernel(seqs, amino, n_first, n_load, *refs):
    srcs, refs = refs[:n_load], refs[n_load:]
    (lefts_out, rights_out, gains, w_in), refs = refs[:4], refs[4:]
    dsts, (g1_ref, win_ref, g2_ref, state, ls, sems) = refs[: n_load - 3], refs[n_load - 3 :]
    dsts = (g1_ref, win_ref, g2_ref) + tuple(dsts)
    copies = [pltpu.make_async_copy(s, d, sems.at[k]) for k, (s, d) in enumerate(zip(srcs, dsts))]
    for copy in copies:
        copy.start()
    for copy in copies[:n_first]:
        copy.wait()
    m_ref, w_out, w_l, w_r = dsts[3:7]
    for step in range(NUM_MODULES):
        for k, g_ref in enumerate((g1_ref, g2_ref)):
            row = g_ref[step : step + 1, :]
            gains[step, k] = jnp.broadcast_to(row, (seqs, row.shape[1])).T
        for k in range(2):
            w_in[step, k] = win_ref[step, k].T * (1.0 if k else 0.5)
    for step in range(NUM_MODULES):
        source = state if step else m_ref
        target = None if step == NUM_MODULES - 1 else state
        msa_module(
            step, seqs, amino, source, gains, w_in, w_out, w_l, w_r, target, lefts_out.at[step], rights_out.at[step], ls
        )
    for copy in copies[n_first:]:
        copy.wait()


def own_call(seqs, amino, load, n_first):
    g1, win, g2, m, w_out, w_l, w_r = load[:7]
    width, feats, hidden = w_l.shape[1], win.shape[2], win.shape[3]
    factor = jax.ShapeDtypeStruct((NUM_MODULES, amino * width, seqs), BF16)
    outs = [
        factor,
        factor,
        jax.ShapeDtypeStruct((NUM_MODULES, 2, feats, seqs), F32),
        jax.ShapeDtypeStruct((NUM_MODULES, 2, hidden, feats), BF16),
    ]
    outs += [jax.ShapeDtypeStruct(x.shape, x.dtype) for x in load[3:]]
    load = [pltpu.with_memory_space_constraint(x, pltpu.HBM) for x in load]
    got = pl.pallas_call(
        functools.partial(own_kernel, seqs, amino, n_first, len(load)),
        out_shape=outs,
        in_specs=[pl.BlockSpec(memory_space=pltpu.HBM)] * len(load),
        out_specs=[pl.BlockSpec(memory_space=pltpu.VMEM)] * len(outs),
        scratch_shapes=[pltpu.VMEM(x.shape, x.dtype) for x in load[:3]]
        + [
            pltpu.VMEM((feats, amino * seqs), F32),
            pltpu.VMEM((amino * width, seqs), F32),
            pltpu.SemaphoreType.DMA((len(load),)),
        ],
        compiler_params=pltpu.CompilerParams(vmem_limit_bytes=VMEM_LIMIT),
        cost_estimate=pl.CostEstimate(flops=4_000_000_000, bytes_accessed=500_000, transcendentals=0),
        name="own",
    )(*load)
    return list(got[:4]), list(got[4:])


def far_kernel(seqs, amino, m_ref, gains, w_in, w_out, w_r, right_out, state):
    for step in range(NUM_MODULES):
        source = state if step else m_ref
        target = None if step == NUM_MODULES - 1 else state
        msa_module(
            step, seqs, amino, source, gains, w_in, w_out, None, w_r, target, None, right_out.at[step], None
        )


def far_call(seqs, amino, m, gains, w_in, w_out, w_r):
    return pl.pallas_call(
        functools.partial(far_kernel, seqs, amino),
        out_shape=jax.ShapeDtypeStruct((NUM_MODULES, amino * w_r.shape[1], seqs), BF16),
        in_specs=[pl.BlockSpec(memory_space=pltpu.VMEM)] * 5,
        out_specs=pl.BlockSpec(memory_space=pltpu.VMEM),
        scratch_shapes=[pltpu.VMEM((w_in.shape[3], amino * seqs), F32)],
        compiler_params=pltpu.CompilerParams(vmem_limit_bytes=VMEM_LIMIT),
        cost_estimate=pl.CostEstimate(flops=3_000_000_000, bytes_accessed=500_000, transcendentals=0),
        name="far",
    )(m, gains, w_in, w_out, w_r)


def swap_groups(parts, width):
    n = len(parts)
    lanes = parts[0].shape[1]
    group = lax.broadcasted_iota(jnp.int32, parts[0].shape, 1) // width
    bit = 1
    while bit < n:
        low = (group & bit) == 0
        shift = bit * width
        new = list(parts)
        for a in range(n):
            if a & bit == 0:
                x, y = parts[a], parts[a | bit]
                new[a] = jnp.where(low, x, pltpu.roll(y, shift, 1))
                new[a | bit] = jnp.where(low, pltpu.roll(x, lanes - shift, 1), y)
        parts = new
        bit *= 2
    return parts


def pair_kernel(first, n_raw, n_col, n_dep, amino, width, depth, n_left, starts, *refs):
    raw, refs = refs[:n_raw], refs[n_raw:]
    lefts, refs = refs[:n_left], refs[n_left:]
    rights, refs = refs[: len(starts)], refs[len(starts) :]
    w_ref, b_ref, keep_ref, send_ref = refs[:4]
    n_right = len(starts)
    per_dep = n_col // n_dep
    pair_ch = w_ref.shape[2]
    groups = LANES // width
    both = 2 * amino
    tiles = amino * width // LANES
    rows_tile = groups * amino
    if first:
        left, ls = refs[4:]
        seqs = ls.shape[3]
        col, dep = lax.axis_index("col"), lax.axis_index("dep")
        for dc in range(n_col):
            source = lax.rem(col - dc + n_col, n_col)
            slot = lax.rem(source - dep * per_dep + n_col, n_col)
            for step in range(NUM_MODULES):
                ls[slot, step] = lefts[dc][step].astype(F32)
        for step in range(NUM_MODULES):
            for u in range(per_dep):
                rows = jnp.concatenate(
                    [ls[u, step].reshape(width, amino, seqs), ls[per_dep + u, step].reshape(width, amino, seqs)],
                    axis=1,
                )
                left[step, u] = rows.reshape(width * both, seqs).astype(BF16)
    else:
        (left,) = lefts
    if raw:
        right, state = refs[4:]
        far_kernel(left.shape[3], amino, *raw, right.at[0], state)
        rights, starts = [right], (0,)
        n_right = 1

    def swapped(outer):
        bigs = []
        for big in range(width // groups):
            first = big * groups
            bigs.append(
                swap_groups([outer[(first + k) * both : (first + k + 1) * both] for k in range(groups)], width)
            )
        return jnp.concatenate([jnp.concatenate([x[k] for x in bigs], axis=1) for k in range(groups)], axis=0)

    items = [
        (step, u, k, t)
        for step in range(NUM_MODULES)
        for u in range(per_dep)
        for k in range(n_right)
        for t in range(tiles)
    ]

    def multiply(step, u, k, t):
        tile = rights[k][starts[k], step, t * LANES : (t + 1) * LANES, :]
        return dot_nt(left[step, u], tile).astype(BF16)

    def finish(step, u, k, t, lhs):
        got = (dot_nn(lhs, w_ref[step]) * (1.0 / depth)).reshape(groups, both, pair_ch)
        rows = slice(t * rows_tile, (t + 1) * rows_tile)
        keep_ref[step, u, k, rows, :] = got[:, :amino].reshape(rows_tile, pair_ch) + b_ref[step : step + 1, :]
        send_ref[step, u, k, rows, :] = got[:, amino:].reshape(rows_tile, pair_ch)

    outer, lhs = multiply(*items[0]), None
    for n in range(len(items) + 1):
        after = multiply(*items[n + 1]) if n + 1 < len(items) else None
        if n >= 1:
            finish(*items[n - 1], lhs)
        if n < len(items):
            lhs = swapped(outer)
        outer = after


def pair_call(name, n_col, n_dep, amino, width, depth, lefts, rights, w, b, raw=()):
    first = len(lefts) > 1
    pair_ch = w.shape[2]
    per_dep = n_col // n_dep
    factors, starts = zip(*rights) if rights else ((), ())
    seqs = lefts[0].shape[-1]
    n_right = max(len(rights), 1)
    out = jax.ShapeDtypeStruct((NUM_MODULES, per_dep, n_right, amino * amino, pair_ch), F32)
    outs, scratch = [out, out], []
    if raw:
        scratch += [
            pltpu.VMEM((1, NUM_MODULES, amino * width, seqs), BF16),
            pltpu.VMEM((raw[2].shape[3], amino * seqs), F32),
        ]
    if first:
        outs.append(jax.ShapeDtypeStruct((NUM_MODULES, per_dep, 2 * amino * width, seqs), BF16))
        scratch.append(pltpu.VMEM((n_col, NUM_MODULES, amino * width, seqs), F32))
    return pl.pallas_call(
        functools.partial(pair_kernel, first, len(raw), n_col, n_dep, amino, width, depth, len(lefts), starts),
        out_shape=outs,
        in_specs=[pl.BlockSpec(memory_space=pltpu.VMEM)] * (len(raw) + len(lefts) + len(factors) + 2),
        out_specs=[pl.BlockSpec(memory_space=pltpu.VMEM)] * len(outs),
        scratch_shapes=scratch,
        compiler_params=pltpu.CompilerParams(vmem_limit_bytes=VMEM_LIMIT),
        cost_estimate=pl.CostEstimate(
            flops=600_000_000 * n_right + (3_000_000_000 if raw else 0), bytes_accessed=1_500_000, transcendentals=0
        ),
        name="pair" + name,
    )(*raw, *lefts, *factors, w, b)


def trans_kernel(last, n_row, n_col, amino, cols, steps, done_steps, *refs):
    n = sum(len(group) for group in steps)
    parts, refs = refs[: 2 * len(steps)], refs[2 * len(steps) :]
    done, refs = refs[: len(done_steps)], refs[len(done_steps) :]
    z_ref, g_ref, win_ref, wout_ref, out_ref = refs
    ratio = n_row // n_col
    row, col = lax.axis_index("row"), lax.axis_index("col")
    per_dep, size = parts[0].shape[1], amino * amino

    def first_column(step):
        off = lax.rem(lax.rem(row, ratio) - step[0] + ratio, ratio)
        return (off * n_col + lax.rem(col - step[1] + n_col, n_col)) * amino

    def places(steps):
        return [
            u * amino * cols + first_column(step) + j
            for u in range(per_dep)
            for step in steps
            for j in range(amino)
        ]

    flat = [step for group in steps for step in group]
    here = places(flat)
    z = jnp.concatenate([z_ref[pl.ds(at, amino, stride=cols), :] for at in here], axis=0)
    for step in range(NUM_MODULES):
        moved = [
            parts[2 * k][step, u, i] + parts[2 * k + 1][step, u, i]
            for u in range(per_dep)
            for k, group in enumerate(steps)
            for i in range(len(group))
        ]
        z = z + jnp.concatenate(moved, axis=0)
        xp = norm_lanes(z, g_ref[step : step + 1, :]).astype(BF16)
        gate = dot_nn(xp, win_ref[step, 0]) * 0.5
        upper = dot_nn(xp, win_ref[step, 1])
        hidden = (silu_of_double(gate) * upper).astype(BF16)
        z = z + dot_nn(hidden, wout_ref[step])
    if last:
        for k, at in enumerate(here):
            out_ref[pl.ds(at, amino, stride=cols), :] = z[k * amino : (k + 1) * amino, :]
        for x, group in zip(done, done_steps):
            for k, at in enumerate(places([step for part in group for step in part])):
                out_ref[pl.ds(at, amino, stride=cols), :] = x[k * amino : (k + 1) * amino, :]
    else:
        out_ref[...] = z


def trans_call(name, last, n_row, n_col, amino, cols, steps, parts, done_steps, done, z, g, win, wout):
    per_dep, pair_ch = parts[0].shape[1], z.shape[1]
    n = sum(len(group) for group in steps)
    shape = z.shape if last else (per_dep * n * amino * amino, pair_ch)
    return pl.pallas_call(
        functools.partial(trans_kernel, last, n_row, n_col, amino, cols, steps, done_steps),
        out_shape=jax.ShapeDtypeStruct(shape, F32),
        in_specs=[pl.BlockSpec(memory_space=pltpu.VMEM)] * (len(parts) + len(done) + 4),
        out_specs=pl.BlockSpec(memory_space=pltpu.VMEM),
        compiler_params=pltpu.CompilerParams(vmem_limit_bytes=VMEM_LIMIT),
        cost_estimate=pl.CostEstimate(flops=1_400_000_000, bytes_accessed=1_500_000, transcendentals=0),
        name="trans" + name,
    )(*parts, *done, z, g, win, wout)


def per_device(n_row, n_col, n_dep, msa, pair, g_ff, w_in, w_out, g_op, w_l, w_r, w_res, b_res, g_pair, p_in, p_out):
    seqs, amino, feats = msa.shape
    width = w_l.shape[2]
    depth = seqs * n_dep
    ratio = n_row // n_col
    cols = amino * n_row
    row, col = lax.axis_index("row"), lax.axis_index("col")

    def rows_by(k):
        return lambda x: lax.ppermute(x, "row", [(r, (r + k) % n_row) for r in range(n_row)])

    def group_by(k):
        pairs = [(r, r // ratio * ratio + (r % ratio + k) % ratio) for r in range(n_row)]
        return lambda x: lax.ppermute(x, "row", pairs)

    def cols_by(k):
        return lambda x: lax.ppermute(x, "col", [(c, (c + k) % n_col) for c in range(n_col)])

    def pick(items, index):
        got = items[0]
        for k in range(1, len(items)):
            got = jnp.where(index == k, items[k], got)
        return got

    def spread_far(right):
        return [right] + [rows_by(k * ratio)(right) for k in range(1, n_col)]

    def moved(x, dr, dc):
        pairs = []
        for r in range(n_row):
            to = r // ratio * ratio + (r % ratio + dr) % ratio
            pairs += [(r * n_col + c, to * n_col + (c + dc) % n_col) for c in range(n_col)]
        return lax.ppermute(x, ("row", "col"), pairs)

    def spread(items):
        group = row // ratio
        wanted = [pick(items, (group - (col + dc) + 2 * n_col) % n_col) for dc in range(n_col)]
        return lambda dr, dc: moved(wanted[dc], dr, dc) if dr or dc else wanted[0]

    w_out, w_l, w_r = (w.transpose(0, 2, 1) for w in (w_out, w_l, w_r))
    m = msa.transpose(1, 2, 0)
    z = pair.reshape(-1, pair.shape[2])
    far = [rows_by(k * ratio)(m) for k in range(1, n_col)]
    load = [g_ff, w_in, g_op, m, w_out, w_l, w_r, w_res, b_res, g_pair, p_in, p_out, z]
    (left, right, gains, w_in), load = own_call(seqs, amino, load, 7)
    m, w_out, w_l, w_r, w_res, b_res, g_pair, p_in, p_out, z = load
    lefts = [left] + [cols_by(dc)(left) for dc in range(1, n_col)]
    others = [(dr, dc) for dr in range(ratio) for dc in range(n_col) if dr or dc]
    others.sort(key=lambda step: (min(step[0], ratio - step[0]) + min(step[1], n_col - step[1])), reverse=True)
    tools = (gains, w_in, w_out, w_r)
    first = (spread([m] + far)(*others[0]), *tools)
    take = spread([right] + [far_call(seqs, amino, x, *tools) for x in far])
    per = -(-(len(others) - 1) // 2)
    steps = [[(0, 0)], others[:1]] + [others[k : k + per] for k in range(1, len(others), per)]
    parts = []
    for k, group in enumerate(steps):
        raw = first if k == 1 else ()
        rights = [] if raw else [(take(*step)[None], 0) for step in group]
        if k > 1:
            lefts, parts[-2] = lax.optimization_barrier((lefts, parts[-2]))
        keep, send, *lead = pair_call(str(k), n_col, n_dep, amino, width, depth, lefts, rights, w_res, b_res, raw)
        lefts = lead or lefts
        parts += [keep, lax.ppermute(send, "dep", [(d, (d + 1) % n_dep) for d in range(n_dep)])]
    call = lambda name, last, *args: trans_call(
        name, last, n_row, n_col, amino, cols, *args, z, g_pair, p_in, p_out
    )
    most = call("0", False, steps[:-1], parts[:-2], [], [])
    z = call("1", True, steps[-1:], parts[-2:], [steps[:-1]], [most])
    return z.reshape(pair.shape)


def solution(mesh):
    return jax.shard_map(
        functools.partial(per_device, mesh.shape["row"], mesh.shape["col"], mesh.shape["dep"]),
        mesh=mesh,
        in_specs=(
            P(("grp", "dep"), ("row", "col"), None),
            P(("grp", "row", "dep"), "col", None),
        )
        + (P(),) * 11,
        out_specs=P(("grp", "row", "dep"), "col", None),
        check_vma=False,
    )
```

```python
import functools

import jax
import jax.numpy as jnp
from jax import lax
from jax.experimental import pallas as pl
from jax.experimental.pallas import tpu as pltpu
from jax.sharding import PartitionSpec as P

NUM_MODULES = 2
LANES = 128
SUB = 8
F32 = jnp.float32
BF16 = jnp.bfloat16
VMEM_LIMIT = 32 * 1024 * 1024


def dot_tn(a, b):
    return lax.dot_general(a, b, (((0,), (0,)), ((), ())), preferred_element_type=F32)


def dot_nt(a, b):
    return lax.dot_general(a, b, (((1,), (1,)), ((), ())), preferred_element_type=F32)


def dot_nn(a, b):
    return lax.dot_general(a, b, (((1,), (0,)), ((), ())), preferred_element_type=F32)


def silu_of_double(x):
    return x * jnp.tanh(x) + x


def norm_rows(m, gain):
    mean = jnp.mean(m, axis=0, keepdims=True)
    centered = m - mean
    var = jnp.mean(centered * centered, axis=0, keepdims=True)
    return centered * lax.rsqrt(var + 1e-05) * gain


def norm_lanes(x, gain):
    mean = jnp.mean(x, axis=1, keepdims=True)
    centered = x - mean
    var = jnp.mean(centered * centered, axis=1, keepdims=True)
    return centered * lax.rsqrt(var + 1e-05) * gain


def msa_module(step, seqs, amino, m_ref, gains, w_in, w_out, w_l, w_r, m_out, left_out, right_out, ls):
    width = w_r.shape[1]
    per = 8
    lanes = per * seqs
    three = len(m_ref.shape) == 3
    gain1 = jnp.concatenate([gains[step, 0]] * per, axis=1)
    gain2 = jnp.concatenate([gains[step, 1]] * per, axis=1)
    for start in range(0, amino, per):
        here = slice(start * seqs, start * seqs + lanes)
        if three:
            m = jnp.concatenate([m_ref[start + k] for k in range(per)], axis=1).astype(F32)
        else:
            m = m_ref[:, here]
        xm = norm_rows(m, gain1).astype(BF16)
        gate = dot_nn(w_in[step, 0], xm)
        upper = dot_nn(w_in[step, 1], xm)
        hidden = (silu_of_double(gate) * upper).astype(BF16)
        m = m + dot_nn(w_out[step], hidden)
        if m_out is not None:
            m_out[:, here] = m
        xo = norm_rows(m, gain2).astype(BF16)
        right = dot_nn(w_r[step], xo)
        if left_out is not None:
            left = dot_nn(w_l[step], xo)
        for k in range(per):
            rows = slice((start + k) * width, (start + k + 1) * width)
            right_out[rows, :] = right[:, k * seqs : (k + 1) * seqs].astype(BF16)
            if left_out is not None:
                ls[rows, :] = left[:, k * seqs : (k + 1) * seqs]
    if left_out is not None:
        for p in range(0, width, 2):
            pair = [ls[pl.ds(p + k, amino, stride=width), :] for k in range(2)]
            left_out[p * amino : (p + 2) * amino, :] = jnp.concatenate(pair, axis=0).astype(BF16)


def own_kernel(seqs, amino, n_first, n_load, *refs):
    srcs, refs = refs[:n_load], refs[n_load:]
    (lefts_out, rights_out, gains, w_in), refs = refs[:4], refs[4:]
    dsts, (g1_ref, win_ref, g2_ref, state, ls, sems) = refs[: n_load - 3], refs[n_load - 3 :]
    dsts = (g1_ref, win_ref, g2_ref) + tuple(dsts)
    copies = [pltpu.make_async_copy(s, d, sems.at[k]) for k, (s, d) in enumerate(zip(srcs, dsts))]
    for copy in copies:
        copy.start()
    for copy in copies[:n_first]:
        copy.wait()
    m_ref, w_out, w_l, w_r = dsts[3:7]
    for step in range(NUM_MODULES):
        for k, g_ref in enumerate((g1_ref, g2_ref)):
            row = g_ref[step : step + 1, :]
            gains[step, k] = jnp.broadcast_to(row, (seqs, row.shape[1])).T
        for k in range(2):
            w_in[step, k] = win_ref[step, k].T * (1.0 if k else 0.5)
    for step in range(NUM_MODULES):
        source = state if step else m_ref
        target = None if step == NUM_MODULES - 1 else state
        msa_module(
            step, seqs, amino, source, gains, w_in, w_out, w_l, w_r, target, lefts_out.at[step], rights_out.at[step], ls
        )
    for copy in copies[n_first:]:
        copy.wait()


def own_call(seqs, amino, load, n_first):
    g1, win, g2, m, w_out, w_l, w_r = load[:7]
    width, feats, hidden = w_l.shape[1], win.shape[2], win.shape[3]
    factor = jax.ShapeDtypeStruct((NUM_MODULES, amino * width, seqs), BF16)
    outs = [
        factor,
        factor,
        jax.ShapeDtypeStruct((NUM_MODULES, 2, feats, seqs), F32),
        jax.ShapeDtypeStruct((NUM_MODULES, 2, hidden, feats), BF16),
    ]
    outs += [jax.ShapeDtypeStruct(x.shape, x.dtype) for x in load[3:]]
    load = [pltpu.with_memory_space_constraint(x, pltpu.HBM) for x in load]
    got = pl.pallas_call(
        functools.partial(own_kernel, seqs, amino, n_first, len(load)),
        out_shape=outs,
        in_specs=[pl.BlockSpec(memory_space=pltpu.HBM)] * len(load),
        out_specs=[pl.BlockSpec(memory_space=pltpu.VMEM)] * len(outs),
        scratch_shapes=[pltpu.VMEM(x.shape, x.dtype) for x in load[:3]]
        + [
            pltpu.VMEM((feats, amino * seqs), F32),
            pltpu.VMEM((amino * width, seqs), F32),
            pltpu.SemaphoreType.DMA((len(load),)),
        ],
        compiler_params=pltpu.CompilerParams(vmem_limit_bytes=VMEM_LIMIT),
        cost_estimate=pl.CostEstimate(flops=4_000_000_000, bytes_accessed=500_000, transcendentals=0),
        name="own",
    )(*load)
    return list(got[:4]), list(got[4:])


def far_kernel(seqs, amino, m_ref, gains, w_in, w_out, w_r, right_out, state):
    for step in range(NUM_MODULES):
        source = state if step else m_ref
        target = None if step == NUM_MODULES - 1 else state
        msa_module(
            step, seqs, amino, source, gains, w_in, w_out, None, w_r, target, None, right_out.at[step], None
        )


def far_call(seqs, amino, m, gains, w_in, w_out, w_r):
    return pl.pallas_call(
        functools.partial(far_kernel, seqs, amino),
        out_shape=jax.ShapeDtypeStruct((NUM_MODULES, amino * w_r.shape[1], seqs), BF16),
        in_specs=[pl.BlockSpec(memory_space=pltpu.VMEM)] * 5,
        out_specs=pl.BlockSpec(memory_space=pltpu.VMEM),
        scratch_shapes=[pltpu.VMEM((w_in.shape[3], amino * seqs), F32)],
        compiler_params=pltpu.CompilerParams(vmem_limit_bytes=VMEM_LIMIT),
        cost_estimate=pl.CostEstimate(flops=3_000_000_000, bytes_accessed=500_000, transcendentals=0),
        name="far",
    )(m, gains, w_in, w_out, w_r)


def swap_groups(parts, width):
    n = len(parts)
    lanes = parts[0].shape[1]
    group = lax.broadcasted_iota(jnp.int32, parts[0].shape, 1) // width
    bit = 1
    while bit < n:
        low = (group & bit) == 0
        shift = bit * width
        new = list(parts)
        for a in range(n):
            if a & bit == 0:
                x, y = parts[a], parts[a | bit]
                new[a] = jnp.where(low, x, pltpu.roll(y, shift, 1))
                new[a | bit] = jnp.where(low, pltpu.roll(x, lanes - shift, 1), y)
        parts = new
        bit *= 2
    return parts


def pair_kernel(first, n_raw, n_col, n_dep, amino, width, depth, n_left, starts, *refs):
    raw, refs = refs[:n_raw], refs[n_raw:]
    lefts, refs = refs[:n_left], refs[n_left:]
    rights, refs = refs[: len(starts)], refs[len(starts) :]
    w_ref, b_ref, keep_ref, send_ref = refs[:4]
    n_right = len(starts)
    per_dep = n_col // n_dep
    pair_ch = w_ref.shape[2]
    groups = LANES // width
    both = 2 * amino
    tiles = amino * width // LANES
    rows_tile = groups * amino
    if first:
        left, ls = refs[4:]
        seqs = ls.shape[3]
        col, dep = lax.axis_index("col"), lax.axis_index("dep")
        for dc in range(n_col):
            source = lax.rem(col - dc + n_col, n_col)
            slot = lax.rem(source - dep * per_dep + n_col, n_col)
            for step in range(NUM_MODULES):
                ls[slot, step] = lefts[dc][step].astype(F32)
        for step in range(NUM_MODULES):
            for u in range(per_dep):
                rows = jnp.concatenate(
                    [ls[u, step].reshape(width, amino, seqs), ls[per_dep + u, step].reshape(width, amino, seqs)],
                    axis=1,
                )
                left[step, u] = rows.reshape(width * both, seqs).astype(BF16)
    else:
        (left,) = lefts
    if raw:
        right, state = refs[4:]
        far_kernel(left.shape[3], amino, *raw, right.at[0], state)
        rights, starts = [right], (0,)
        n_right = 1

    def swapped(outer):
        bigs = []
        for big in range(width // groups):
            first = big * groups
            bigs.append(
                swap_groups([outer[(first + k) * both : (first + k + 1) * both] for k in range(groups)], width)
            )
        return jnp.concatenate([jnp.concatenate([x[k] for x in bigs], axis=1) for k in range(groups)], axis=0)

    items = [
        (step, u, k, t)
        for step in range(NUM_MODULES)
        for u in range(per_dep)
        for k in range(n_right)
        for t in range(tiles)
    ]

    def multiply(step, u, k, t):
        tile = rights[k][starts[k], step, t * LANES : (t + 1) * LANES, :]
        return dot_nt(left[step, u], tile).astype(BF16)

    def finish(step, u, k, t, lhs):
        got = (dot_nn(lhs, w_ref[step]) * (1.0 / depth)).reshape(groups, both, pair_ch)
        rows = slice(t * rows_tile, (t + 1) * rows_tile)
        keep_ref[step, u, k, rows, :] = got[:, :amino].reshape(rows_tile, pair_ch) + b_ref[step : step + 1, :]
        send_ref[step, u, k, rows, :] = got[:, amino:].reshape(rows_tile, pair_ch)

    outer, lhs = multiply(*items[0]), None
    for n in range(len(items) + 1):
        after = multiply(*items[n + 1]) if n + 1 < len(items) else None
        if n >= 1:
            finish(*items[n - 1], lhs)
        if n < len(items):
            lhs = swapped(outer)
        outer = after


def pair_call(name, n_col, n_dep, amino, width, depth, lefts, rights, w, b, raw=()):
    first = len(lefts) > 1
    pair_ch = w.shape[2]
    per_dep = n_col // n_dep
    factors, starts = zip(*rights) if rights else ((), ())
    seqs = lefts[0].shape[-1]
    n_right = max(len(rights), 1)
    out = jax.ShapeDtypeStruct((NUM_MODULES, per_dep, n_right, amino * amino, pair_ch), F32)
    outs, scratch = [out, out], []
    if raw:
        scratch += [
            pltpu.VMEM((1, NUM_MODULES, amino * width, seqs), BF16),
            pltpu.VMEM((raw[2].shape[3], amino * seqs), F32),
        ]
    if first:
        outs.append(jax.ShapeDtypeStruct((NUM_MODULES, per_dep, 2 * amino * width, seqs), BF16))
        scratch.append(pltpu.VMEM((n_col, NUM_MODULES, amino * width, seqs), F32))
    return pl.pallas_call(
        functools.partial(pair_kernel, first, len(raw), n_col, n_dep, amino, width, depth, len(lefts), starts),
        out_shape=outs,
        in_specs=[pl.BlockSpec(memory_space=pltpu.VMEM)] * (len(raw) + len(lefts) + len(factors) + 2),
        out_specs=[pl.BlockSpec(memory_space=pltpu.VMEM)] * len(outs),
        scratch_shapes=scratch,
        compiler_params=pltpu.CompilerParams(vmem_limit_bytes=VMEM_LIMIT),
        cost_estimate=pl.CostEstimate(
            flops=1_000_000, bytes_accessed=1000, transcendentals=0
        ),
        name="pair" + name,
    )(*raw, *lefts, *factors, w, b)


def trans_kernel(last, n_row, n_col, amino, cols, steps, done_steps, *refs):
    n = sum(len(group) for group in steps)
    parts, refs = refs[: 2 * len(steps)], refs[2 * len(steps) :]
    done, refs = refs[: len(done_steps)], refs[len(done_steps) :]
    z_ref, g_ref, win_ref, wout_ref, out_ref = refs
    ratio = n_row // n_col
    row, col = lax.axis_index("row"), lax.axis_index("col")
    per_dep, size = parts[0].shape[1], amino * amino

    def first_column(step):
        off = lax.rem(lax.rem(row, ratio) - step[0] + ratio, ratio)
        return (off * n_col + lax.rem(col - step[1] + n_col, n_col)) * amino

    def places(steps):
        return [
            u * amino * cols + first_column(step) + j
            for u in range(per_dep)
            for step in steps
            for j in range(amino)
        ]

    flat = [step for group in steps for step in group]
    here = places(flat)
    z = jnp.concatenate([z_ref[pl.ds(at, amino, stride=cols), :] for at in here], axis=0)
    for step in range(NUM_MODULES):
        moved = [
            parts[2 * k][step, u, i] + parts[2 * k + 1][step, u, i]
            for u in range(per_dep)
            for k, group in enumerate(steps)
            for i in range(len(group))
        ]
        z = z + jnp.concatenate(moved, axis=0)
        xp = norm_lanes(z, g_ref[step : step + 1, :]).astype(BF16)
        gate = dot_nn(xp, win_ref[step, 0]) * 0.5
        upper = dot_nn(xp, win_ref[step, 1])
        hidden = (silu_of_double(gate) * upper).astype(BF16)
        z = z + dot_nn(hidden, wout_ref[step])
    if last:
        for k, at in enumerate(here):
            out_ref[pl.ds(at, amino, stride=cols), :] = z[k * amino : (k + 1) * amino, :]
        for x, group in zip(done, done_steps):
            for k, at in enumerate(places([step for part in group for step in part])):
                out_ref[pl.ds(at, amino, stride=cols), :] = x[k * amino : (k + 1) * amino, :]
    else:
        out_ref[...] = z


def trans_call(name, last, n_row, n_col, amino, cols, steps, parts, done_steps, done, z, g, win, wout):
    per_dep, pair_ch = parts[0].shape[1], z.shape[1]
    n = sum(len(group) for group in steps)
    shape = z.shape if last else (per_dep * n * amino * amino, pair_ch)
    return pl.pallas_call(
        functools.partial(trans_kernel, last, n_row, n_col, amino, cols, steps, done_steps),
        out_shape=jax.ShapeDtypeStruct(shape, F32),
        in_specs=[pl.BlockSpec(memory_space=pltpu.VMEM)] * (len(parts) + len(done) + 4),
        out_specs=pl.BlockSpec(memory_space=pltpu.VMEM),
        compiler_params=pltpu.CompilerParams(vmem_limit_bytes=VMEM_LIMIT),
        cost_estimate=pl.CostEstimate(flops=1_400_000_000, bytes_accessed=1_500_000, transcendentals=0),
        name="trans" + name,
    )(*parts, *done, z, g, win, wout)


def per_device(n_row, n_col, n_dep, msa, pair, g_ff, w_in, w_out, g_op, w_l, w_r, w_res, b_res, g_pair, p_in, p_out):
    seqs, amino, feats = msa.shape
    width = w_l.shape[2]
    depth = seqs * n_dep
    ratio = n_row // n_col
    cols = amino * n_row
    row, col = lax.axis_index("row"), lax.axis_index("col")

    def rows_by(k):
        return lambda x: lax.ppermute(x, "row", [(r, (r + k) % n_row) for r in range(n_row)])

    def group_by(k):
        pairs = [(r, r // ratio * ratio + (r % ratio + k) % ratio) for r in range(n_row)]
        return lambda x: lax.ppermute(x, "row", pairs)

    def cols_by(k):
        return lambda x: lax.ppermute(x, "col", [(c, (c + k) % n_col) for c in range(n_col)])

    def pick(items, index):
        got = items[0]
        for k in range(1, len(items)):
            got = jnp.where(index == k, items[k], got)
        return got

    def spread_far(right):
        return [right] + [rows_by(k * ratio)(right) for k in range(1, n_col)]

    def moved(x, dr, dc):
        pairs = []
        for r in range(n_row):
            to = r // ratio * ratio + (r % ratio + dr) % ratio
            pairs += [(r * n_col + c, to * n_col + (c + dc) % n_col) for c in range(n_col)]
        return lax.ppermute(x, ("row", "col"), pairs)

    def spread(items):
        group = row // ratio
        wanted = [pick(items, (group - (col + dc) + 2 * n_col) % n_col) for dc in range(n_col)]
        return lambda dr, dc: moved(wanted[dc], dr, dc) if dr or dc else wanted[0]

    w_out, w_l, w_r = (w.transpose(0, 2, 1) for w in (w_out, w_l, w_r))
    m = msa.transpose(1, 2, 0)
    z = pair.reshape(-1, pair.shape[2])
    far = [rows_by(k * ratio)(m) for k in range(1, n_col)]
    load = [g_ff, w_in, g_op, m, w_out, w_l, w_r, w_res, b_res, g_pair, p_in, p_out, z]
    (left, right, gains, w_in), load = own_call(seqs, amino, load, 7)
    m, w_out, w_l, w_r, w_res, b_res, g_pair, p_in, p_out, z = load
    lefts = [left] + [cols_by(dc)(left) for dc in range(1, n_col)]
    others = [(dr, dc) for dr in range(ratio) for dc in range(n_col) if dr or dc]
    others.sort(key=lambda step: (min(step[0], ratio - step[0]) + min(step[1], n_col - step[1])), reverse=True)
    tools = (gains, w_in, w_out, w_r)
    first = (spread([m] + far)(*others[0]), *tools)
    take = spread([right] + [far_call(seqs, amino, x, *tools) for x in far])
    per = len(others) - 1 if ratio * n_col <= 4 else n_col
    steps = [[(0, 0)], others[:1]] + [others[k : k + per] for k in range(1, len(others), per)]
    parts = []
    for k, group in enumerate(steps):
        raw = first if k == 1 else ()
        rights = [] if raw else [(take(*step)[None], 0) for step in group]
        if k > 1:
            lefts, parts[-2] = lax.optimization_barrier((lefts, parts[-2]))
        keep, send, *lead = pair_call(str(k), n_col, n_dep, amino, width, depth, lefts, rights, w_res, b_res, raw)
        lefts = lead or lefts
        parts += [keep, lax.ppermute(send, "dep", [(d, (d + 1) % n_dep) for d in range(n_dep)])]
    call = lambda name, last, *args: trans_call(
        name, last, n_row, n_col, amino, cols, *args, z, g_pair, p_in, p_out
    )
    most = call("0", False, steps[:-1], parts[:-2], [], [])
    z = call("1", True, steps[-1:], parts[-2:], [steps[:-1]], [most])
    return z.reshape(pair.shape)


def solution(mesh):
    return jax.shard_map(
        functools.partial(per_device, mesh.shape["row"], mesh.shape["col"], mesh.shape["dep"]),
        mesh=mesh,
        in_specs=(
            P(("grp", "dep"), ("row", "col"), None),
            P(("grp", "row", "dep"), "col", None),
        )
        + (P(),) * 11,
        out_specs=P(("grp", "row", "dep"), "col", None),
        check_vma=False,
    )
```

```python
import functools

import jax
import jax.numpy as jnp
from jax import lax
from jax.experimental import pallas as pl
from jax.experimental.pallas import tpu as pltpu
from jax.sharding import PartitionSpec as P

NUM_MODULES = 2
LANES = 128
SUB = 8
F32 = jnp.float32
BF16 = jnp.bfloat16
VMEM_LIMIT = 32 * 1024 * 1024


def dot_tn(a, b):
    return lax.dot_general(a, b, (((0,), (0,)), ((), ())), preferred_element_type=F32)


def dot_nt(a, b):
    return lax.dot_general(a, b, (((1,), (1,)), ((), ())), preferred_element_type=F32)


def dot_nn(a, b):
    return lax.dot_general(a, b, (((1,), (0,)), ((), ())), preferred_element_type=F32)


def silu_of_double(x):
    return x * jnp.tanh(x) + x


def norm_rows(m, gain):
    mean = jnp.mean(m, axis=0, keepdims=True)
    centered = m - mean
    var = jnp.mean(centered * centered, axis=0, keepdims=True)
    return centered * lax.rsqrt(var + 1e-05) * gain


def norm_lanes(x, gain):
    mean = jnp.mean(x, axis=1, keepdims=True)
    centered = x - mean
    var = jnp.mean(centered * centered, axis=1, keepdims=True)
    return centered * lax.rsqrt(var + 1e-05) * gain


def msa_module(step, seqs, amino, m_ref, gains, w_in, w_out, w_l, w_r, m_out, left_out, right_out, ls):
    width = w_r.shape[1]
    per = 8
    lanes = per * seqs
    three = len(m_ref.shape) == 3
    gain1 = jnp.concatenate([gains[step, 0]] * per, axis=1)
    gain2 = jnp.concatenate([gains[step, 1]] * per, axis=1)
    for start in range(0, amino, per):
        here = slice(start * seqs, start * seqs + lanes)
        if three:
            m = jnp.concatenate([m_ref[start + k] for k in range(per)], axis=1).astype(F32)
        else:
            m = m_ref[:, here]
        xm = norm_rows(m, gain1).astype(BF16)
        gate = dot_nn(w_in[step, 0], xm)
        upper = dot_nn(w_in[step, 1], xm)
        hidden = (silu_of_double(gate) * upper).astype(BF16)
        m = m + dot_nn(w_out[step], hidden)
        if m_out is not None:
            m_out[:, here] = m
        xo = norm_rows(m, gain2).astype(BF16)
        right = dot_nn(w_r[step], xo)
        if left_out is not None:
            left = dot_nn(w_l[step], xo)
        for k in range(per):
            rows = slice((start + k) * width, (start + k + 1) * width)
            right_out[rows, :] = right[:, k * seqs : (k + 1) * seqs].astype(BF16)
            if left_out is not None:
                ls[rows, :] = left[:, k * seqs : (k + 1) * seqs]
    if left_out is not None:
        for p in range(0, width, 2):
            pair = [ls[pl.ds(p + k, amino, stride=width), :] for k in range(2)]
            left_out[p * amino : (p + 2) * amino, :] = jnp.concatenate(pair, axis=0).astype(BF16)


def own_kernel(seqs, amino, n_first, n_load, *refs):
    srcs, refs = refs[:n_load], refs[n_load:]
    (lefts_out, rights_out, gains, w_in), refs = refs[:4], refs[4:]
    dsts, (g1_ref, win_ref, g2_ref, state, ls, sems) = refs[: n_load - 3], refs[n_load - 3 :]
    dsts = (g1_ref, win_ref, g2_ref) + tuple(dsts)
    copies = [pltpu.make_async_copy(s, d, sems.at[k]) for k, (s, d) in enumerate(zip(srcs, dsts))]
    for copy in copies:
        copy.start()
    for copy in copies[:n_first]:
        copy.wait()
    m_ref, w_out, w_l, w_r = dsts[3:7]
    for step in range(NUM_MODULES):
        for k, g_ref in enumerate((g1_ref, g2_ref)):
            row = g_ref[step : step + 1, :]
            gains[step, k] = jnp.broadcast_to(row, (seqs, row.shape[1])).T
        for k in range(2):
            w_in[step, k] = win_ref[step, k].T * (1.0 if k else 0.5)
    for step in range(NUM_MODULES):
        source = state if step else m_ref
        target = None if step == NUM_MODULES - 1 else state
        msa_module(
            step, seqs, amino, source, gains, w_in, w_out, w_l, w_r, target, lefts_out.at[step], rights_out.at[step], ls
        )
    for copy in copies[n_first:]:
        copy.wait()


def own_call(seqs, amino, load, n_first):
    g1, win, g2, m, w_out, w_l, w_r = load[:7]
    width, feats, hidden = w_l.shape[1], win.shape[2], win.shape[3]
    factor = jax.ShapeDtypeStruct((NUM_MODULES, amino * width, seqs), BF16)
    outs = [
        factor,
        factor,
        jax.ShapeDtypeStruct((NUM_MODULES, 2, feats, seqs), F32),
        jax.ShapeDtypeStruct((NUM_MODULES, 2, hidden, feats), BF16),
    ]
    outs += [jax.ShapeDtypeStruct(x.shape, x.dtype) for x in load[3:]]
    load = [pltpu.with_memory_space_constraint(x, pltpu.HBM) for x in load]
    got = pl.pallas_call(
        functools.partial(own_kernel, seqs, amino, n_first, len(load)),
        out_shape=outs,
        in_specs=[pl.BlockSpec(memory_space=pltpu.HBM)] * len(load),
        out_specs=[pl.BlockSpec(memory_space=pltpu.VMEM)] * len(outs),
        scratch_shapes=[pltpu.VMEM(x.shape, x.dtype) for x in load[:3]]
        + [
            pltpu.VMEM((feats, amino * seqs), F32),
            pltpu.VMEM((amino * width, seqs), F32),
            pltpu.SemaphoreType.DMA((len(load),)),
        ],
        compiler_params=pltpu.CompilerParams(vmem_limit_bytes=VMEM_LIMIT),
        cost_estimate=pl.CostEstimate(flops=4_000_000_000, bytes_accessed=500_000, transcendentals=0),
        name="own",
    )(*load)
    return list(got[:4]), list(got[4:])


def far_kernel(seqs, amino, m_ref, gains, w_in, w_out, w_r, right_out, state):
    for step in range(NUM_MODULES):
        source = state if step else m_ref
        target = None if step == NUM_MODULES - 1 else state
        msa_module(
            step, seqs, amino, source, gains, w_in, w_out, None, w_r, target, None, right_out.at[step], None
        )


def far_call(seqs, amino, m, gains, w_in, w_out, w_r):
    return pl.pallas_call(
        functools.partial(far_kernel, seqs, amino),
        out_shape=jax.ShapeDtypeStruct((NUM_MODULES, amino * w_r.shape[1], seqs), BF16),
        in_specs=[pl.BlockSpec(memory_space=pltpu.VMEM)] * 5,
        out_specs=pl.BlockSpec(memory_space=pltpu.VMEM),
        scratch_shapes=[pltpu.VMEM((w_in.shape[3], amino * seqs), F32)],
        compiler_params=pltpu.CompilerParams(vmem_limit_bytes=VMEM_LIMIT),
        cost_estimate=pl.CostEstimate(flops=3_000_000_000, bytes_accessed=500_000, transcendentals=0),
        name="far",
    )(m, gains, w_in, w_out, w_r)


def swap_groups(parts, width):
    n = len(parts)
    lanes = parts[0].shape[1]
    group = lax.broadcasted_iota(jnp.int32, parts[0].shape, 1) // width
    bit = 1
    while bit < n:
        low = (group & bit) == 0
        shift = bit * width
        new = list(parts)
        for a in range(n):
            if a & bit == 0:
                x, y = parts[a], parts[a | bit]
                new[a] = jnp.where(low, x, pltpu.roll(y, shift, 1))
                new[a | bit] = jnp.where(low, pltpu.roll(x, lanes - shift, 1), y)
        parts = new
        bit *= 2
    return parts


def pair_kernel(first, n_raw, n_col, n_dep, amino, width, depth, n_left, starts, *refs):
    raw, refs = refs[:n_raw], refs[n_raw:]
    lefts, refs = refs[:n_left], refs[n_left:]
    rights, refs = refs[: len(starts)], refs[len(starts) :]
    w_ref, b_ref, keep_ref, send_ref = refs[:4]
    n_right = len(starts)
    per_dep = n_col // n_dep
    pair_ch = w_ref.shape[2]
    groups = LANES // width
    both = 2 * amino
    tiles = amino * width // LANES
    rows_tile = groups * amino
    if first:
        left, ls = refs[4:]
        seqs = ls.shape[3]
        col, dep = lax.axis_index("col"), lax.axis_index("dep")
        for dc in range(n_col):
            source = lax.rem(col - dc + n_col, n_col)
            slot = lax.rem(source - dep * per_dep + n_col, n_col)
            for step in range(NUM_MODULES):
                ls[slot, step] = lefts[dc][step].astype(F32)
        for step in range(NUM_MODULES):
            for u in range(per_dep):
                rows = jnp.concatenate(
                    [ls[u, step].reshape(width, amino, seqs), ls[per_dep + u, step].reshape(width, amino, seqs)],
                    axis=1,
                )
                left[step, u] = rows.reshape(width * both, seqs).astype(BF16)
    else:
        (left,) = lefts
    if raw:
        right, state = refs[4:]
        far_kernel(left.shape[3], amino, *raw, right.at[0], state)
        rights, starts = [right], (0,)
        n_right = 1

    def swapped(outer):
        bigs = []
        for big in range(width // groups):
            first = big * groups
            bigs.append(
                swap_groups([outer[(first + k) * both : (first + k + 1) * both] for k in range(groups)], width)
            )
        return jnp.concatenate([jnp.concatenate([x[k] for x in bigs], axis=1) for k in range(groups)], axis=0)

    items = [
        (step, u, k, t)
        for step in range(NUM_MODULES)
        for u in range(per_dep)
        for k in range(n_right)
        for t in range(tiles)
    ]

    def multiply(step, u, k, t):
        tile = rights[k][starts[k], step, t * LANES : (t + 1) * LANES, :]
        return dot_nt(left[step, u], tile).astype(BF16)

    def finish(step, u, k, t, lhs):
        got = (dot_nn(lhs, w_ref[step]) * (1.0 / depth)).reshape(groups, both, pair_ch)
        rows = slice(t * rows_tile, (t + 1) * rows_tile)
        keep_ref[step, u, k, rows, :] = got[:, :amino].reshape(rows_tile, pair_ch) + b_ref[step : step + 1, :]
        send_ref[step, u, k, rows, :] = got[:, amino:].reshape(rows_tile, pair_ch)

    outer, lhs = multiply(*items[0]), None
    for n in range(len(items) + 1):
        after = multiply(*items[n + 1]) if n + 1 < len(items) else None
        if n >= 1:
            finish(*items[n - 1], lhs)
        if n < len(items):
            lhs = swapped(outer)
        outer = after


def pair_call(name, n_col, n_dep, amino, width, depth, lefts, rights, w, b, raw=()):
    first = len(lefts) > 1
    pair_ch = w.shape[2]
    per_dep = n_col // n_dep
    factors, starts = zip(*rights) if rights else ((), ())
    seqs = lefts[0].shape[-1]
    n_right = max(len(rights), 1)
    out = jax.ShapeDtypeStruct((NUM_MODULES, per_dep, n_right, amino * amino, pair_ch), F32)
    outs, scratch = [out, out], []
    if raw:
        scratch += [
            pltpu.VMEM((1, NUM_MODULES, amino * width, seqs), BF16),
            pltpu.VMEM((raw[2].shape[3], amino * seqs), F32),
        ]
    if first:
        outs.append(jax.ShapeDtypeStruct((NUM_MODULES, per_dep, 2 * amino * width, seqs), BF16))
        scratch.append(pltpu.VMEM((n_col, NUM_MODULES, amino * width, seqs), F32))
    return pl.pallas_call(
        functools.partial(pair_kernel, first, len(raw), n_col, n_dep, amino, width, depth, len(lefts), starts),
        out_shape=outs,
        in_specs=[pl.BlockSpec(memory_space=pltpu.VMEM)] * (len(raw) + len(lefts) + len(factors) + 2),
        out_specs=[pl.BlockSpec(memory_space=pltpu.VMEM)] * len(outs),
        scratch_shapes=scratch,
        compiler_params=pltpu.CompilerParams(vmem_limit_bytes=VMEM_LIMIT),
        cost_estimate=pl.CostEstimate(
            flops=1_000_000, bytes_accessed=1000, transcendentals=0
        ),
        name="pair" + name,
    )(*raw, *lefts, *factors, w, b)


def trans_kernel(last, n_row, n_col, amino, cols, steps, next_steps, *refs):
    parts, refs = refs[: 2 * len(steps)], refs[2 * len(steps) :]
    if last:
        start_ref, done_ref, g_ref, win_ref, wout_ref, out_ref = refs
    else:
        next_ref, z_ref, g_ref, win_ref, wout_ref, out_ref, after_ref = refs
    ratio = n_row // n_col
    row, col = lax.axis_index("row"), lax.axis_index("col")
    per_dep = parts[0].shape[1]

    def places(steps):
        found = []
        for u in range(per_dep):
            for dr, dc in steps:
                off = lax.rem(lax.rem(row, ratio) - dr + ratio, ratio)
                first = (off * n_col + lax.rem(col - dc + n_col, n_col)) * amino
                found += [u * amino * cols + first + j for j in range(amino)]
        return found

    def gather(steps):
        return jnp.concatenate([z_ref[pl.ds(at, amino, stride=cols), :] for at in places(steps)], axis=0)

    def blocks(step, refs):
        return jnp.concatenate(
            [
                functools.reduce(jnp.add, [ref[step, u, i] for ref in group])
                for u in range(per_dep)
                for group in refs
                for i in range(group[0].shape[2])
            ],
            axis=0,
        )

    flat = [step for group in steps for step in group]
    if last:
        z = start_ref[...]
        out_ref[...] = done_ref[...]
    else:
        z = gather(flat)
        after_ref[...] = gather(next_steps) + blocks(0, [(next_ref,)])
    for step in range(NUM_MODULES):
        pairs = [(parts[2 * k], parts[2 * k + 1]) for k in range(len(steps))]
        if last and step == 0:
            pairs = [x[1:] for x in pairs]
        z = z + blocks(step, pairs)
        xp = norm_lanes(z, g_ref[step : step + 1, :]).astype(BF16)
        gate = dot_nn(xp, win_ref[step, 0]) * 0.5
        upper = dot_nn(xp, win_ref[step, 1])
        hidden = (silu_of_double(gate) * upper).astype(BF16)
        z = z + dot_nn(hidden, wout_ref[step])
    for k, at in enumerate(places(flat)):
        out_ref[pl.ds(at, amino, stride=cols), :] = z[k * amino : (k + 1) * amino, :]


def trans_call(name, last, n_row, n_col, amino, cols, steps, parts, next_steps, ins, g, win, wout):
    per_dep, pair_ch = parts[0].shape[1], g.shape[1]
    outs = [jax.ShapeDtypeStruct((per_dep * amino * cols, pair_ch), F32)]
    if not last:
        outs.append(jax.ShapeDtypeStruct((per_dep * len(next_steps) * amino * amino, pair_ch), F32))
    return pl.pallas_call(
        functools.partial(trans_kernel, last, n_row, n_col, amino, cols, steps, next_steps),
        out_shape=outs,
        in_specs=[pl.BlockSpec(memory_space=pltpu.VMEM)] * (len(parts) + len(ins) + 3),
        out_specs=[pl.BlockSpec(memory_space=pltpu.VMEM)] * len(outs),
        compiler_params=pltpu.CompilerParams(vmem_limit_bytes=VMEM_LIMIT),
        cost_estimate=pl.CostEstimate(flops=1_400_000_000, bytes_accessed=1_500_000, transcendentals=0),
        name="trans" + name,
    )(*parts, *ins, g, win, wout)


def per_device(n_row, n_col, n_dep, msa, pair, g_ff, w_in, w_out, g_op, w_l, w_r, w_res, b_res, g_pair, p_in, p_out):
    seqs, amino, feats = msa.shape
    width = w_l.shape[2]
    depth = seqs * n_dep
    ratio = n_row // n_col
    cols = amino * n_row
    row, col = lax.axis_index("row"), lax.axis_index("col")

    def rows_by(k):
        return lambda x: lax.ppermute(x, "row", [(r, (r + k) % n_row) for r in range(n_row)])

    def group_by(k):
        pairs = [(r, r // ratio * ratio + (r % ratio + k) % ratio) for r in range(n_row)]
        return lambda x: lax.ppermute(x, "row", pairs)

    def cols_by(k):
        return lambda x: lax.ppermute(x, "col", [(c, (c + k) % n_col) for c in range(n_col)])

    def pick(items, index):
        got = items[0]
        for k in range(1, len(items)):
            got = jnp.where(index == k, items[k], got)
        return got

    def spread_far(right):
        return [right] + [rows_by(k * ratio)(right) for k in range(1, n_col)]

    def moved(x, dr, dc):
        pairs = []
        for r in range(n_row):
            to = r // ratio * ratio + (r % ratio + dr) % ratio
            pairs += [(r * n_col + c, to * n_col + (c + dc) % n_col) for c in range(n_col)]
        return lax.ppermute(x, ("row", "col"), pairs)

    def spread(items):
        group = row // ratio
        wanted = [pick(items, (group - (col + dc) + 2 * n_col) % n_col) for dc in range(n_col)]
        return lambda dr, dc: moved(wanted[dc], dr, dc) if dr or dc else wanted[0]

    w_out, w_l, w_r = (w.transpose(0, 2, 1) for w in (w_out, w_l, w_r))
    m = msa.transpose(1, 2, 0)
    z = pair.reshape(-1, pair.shape[2])
    far = [rows_by(k * ratio)(m) for k in range(1, n_col)]
    load = [g_ff, w_in, g_op, m, w_out, w_l, w_r, w_res, b_res, g_pair, p_in, p_out, z]
    (left, right, gains, w_in), load = own_call(seqs, amino, load, 7)
    m, w_out, w_l, w_r, w_res, b_res, g_pair, p_in, p_out, z = load
    lefts = [left] + [cols_by(dc)(left) for dc in range(1, n_col)]
    others = [(dr, dc) for dr in range(ratio) for dc in range(n_col) if dr or dc]
    others.sort(key=lambda step: (min(step[0], ratio - step[0]) + min(step[1], n_col - step[1])), reverse=True)
    tools = (gains, w_in, w_out, w_r)
    first = (spread([m] + far)(*others[0]), *tools)
    take = spread([right] + [far_call(seqs, amino, x, *tools) for x in far])
    per = len(others) - 1 if ratio * n_col <= 4 else n_col
    steps = [[(0, 0)], others[:1]] + [others[k : k + per] for k in range(1, len(others), per)]
    parts = []
    for k, group in enumerate(steps):
        raw = first if k == 1 else ()
        rights = [] if raw else [(take(*step)[None], 0) for step in group]
        if k > 1:
            lefts, parts[-2] = lax.optimization_barrier((lefts, parts[-2]))
        keep, send, *lead = pair_call(str(k), n_col, n_dep, amino, width, depth, lefts, rights, w_res, b_res, raw)
        lefts = lead or lefts
        parts += [keep, lax.ppermute(send, "dep", [(d, (d + 1) % n_dep) for d in range(n_dep)])]
    call = lambda name, last, *args: trans_call(
        name, last, n_row, n_col, amino, cols, *args, g_pair, p_in, p_out
    )
    most, start = call("0", False, steps[:-1], parts[:-2], steps[-1], [parts[-2], z])
    (z,) = call("1", True, steps[-1:], parts[-2:], [], [start, most])
    return z.reshape(pair.shape)


def solution(mesh):
    return jax.shard_map(
        functools.partial(per_device, mesh.shape["row"], mesh.shape["col"], mesh.shape["dep"]),
        mesh=mesh,
        in_specs=(
            P(("grp", "dep"), ("row", "col"), None),
            P(("grp", "row", "dep"), "col", None),
        )
        + (P(),) * 11,
        out_specs=P(("grp", "row", "dep"), "col", None),
        check_vma=False,
    )
```

```python
import functools

import jax
import jax.numpy as jnp
from jax import lax
from jax.experimental import pallas as pl
from jax.experimental.pallas import tpu as pltpu
from jax.sharding import PartitionSpec as P

NUM_MODULES = 2
LANES = 128
SUB = 8
F32 = jnp.float32
BF16 = jnp.bfloat16
VMEM_LIMIT = 32 * 1024 * 1024


def dot_tn(a, b):
    return lax.dot_general(a, b, (((0,), (0,)), ((), ())), preferred_element_type=F32)


def dot_nt(a, b):
    return lax.dot_general(a, b, (((1,), (1,)), ((), ())), preferred_element_type=F32)


def dot_nn(a, b):
    return lax.dot_general(a, b, (((1,), (0,)), ((), ())), preferred_element_type=F32)


def silu_of_double(x):
    return x * jnp.tanh(x) + x


def norm_rows(m, gain):
    mean = jnp.mean(m, axis=0, keepdims=True)
    centered = m - mean
    var = jnp.mean(centered * centered, axis=0, keepdims=True)
    return centered * lax.rsqrt(var + 1e-05) * gain


def norm_lanes(x, gain):
    mean = jnp.mean(x, axis=1, keepdims=True)
    centered = x - mean
    var = jnp.mean(centered * centered, axis=1, keepdims=True)
    return centered * lax.rsqrt(var + 1e-05) * gain


def msa_module(step, seqs, amino, m_ref, gains, w_in, w_out, w_l, w_r, m_out, left_out, right_out, ls):
    width = w_r.shape[1]
    per = 8
    lanes = per * seqs
    three = len(m_ref.shape) == 3
    gain1 = jnp.concatenate([gains[step, 0]] * per, axis=1)
    gain2 = jnp.concatenate([gains[step, 1]] * per, axis=1)
    for start in range(0, amino, per):
        here = slice(start * seqs, start * seqs + lanes)
        if three:
            m = jnp.concatenate([m_ref[start + k] for k in range(per)], axis=1).astype(F32)
        else:
            m = m_ref[:, here]
        xm = norm_rows(m, gain1).astype(BF16)
        gate = dot_nn(w_in[step, 0], xm)
        upper = dot_nn(w_in[step, 1], xm)
        hidden = (silu_of_double(gate) * upper).astype(BF16)
        m = m + dot_nn(w_out[step], hidden)
        if m_out is not None:
            m_out[:, here] = m
        xo = norm_rows(m, gain2).astype(BF16)
        right = dot_nn(w_r[step], xo)
        if left_out is not None:
            left = dot_nn(w_l[step], xo)
        for k in range(per):
            rows = slice((start + k) * width, (start + k + 1) * width)
            right_out[rows, :] = right[:, k * seqs : (k + 1) * seqs].astype(BF16)
            if left_out is not None:
                ls[rows, :] = left[:, k * seqs : (k + 1) * seqs]
    if left_out is not None:
        for p in range(0, width, 2):
            pair = [ls[pl.ds(p + k, amino, stride=width), :] for k in range(2)]
            left_out[p * amino : (p + 2) * amino, :] = jnp.concatenate(pair, axis=0).astype(BF16)


def own_kernel(seqs, amino, n_first, n_load, *refs):
    srcs, refs = refs[:n_load], refs[n_load:]
    (lefts_out, rights_out, gains, w_in), refs = refs[:4], refs[4:]
    dsts, (g1_ref, win_ref, g2_ref, state, ls, sems) = refs[: n_load - 3], refs[n_load - 3 :]
    dsts = (g1_ref, win_ref, g2_ref) + tuple(dsts)
    copies = [pltpu.make_async_copy(s, d, sems.at[k]) for k, (s, d) in enumerate(zip(srcs, dsts))]
    for copy in copies:
        copy.start()
    for copy in copies[:n_first]:
        copy.wait()
    m_ref, w_out, w_l, w_r = dsts[3:7]
    for step in range(NUM_MODULES):
        for k, g_ref in enumerate((g1_ref, g2_ref)):
            row = g_ref[step : step + 1, :]
            gains[step, k] = jnp.broadcast_to(row, (seqs, row.shape[1])).T
        for k in range(2):
            w_in[step, k] = win_ref[step, k].T * (1.0 if k else 0.5)
    for step in range(NUM_MODULES):
        source = state if step else m_ref
        target = None if step == NUM_MODULES - 1 else state
        msa_module(
            step, seqs, amino, source, gains, w_in, w_out, w_l, w_r, target, lefts_out.at[step], rights_out.at[step], ls
        )
    for copy in copies[n_first:]:
        copy.wait()


def own_call(seqs, amino, load, n_first):
    g1, win, g2, m, w_out, w_l, w_r = load[:7]
    width, feats, hidden = w_l.shape[1], win.shape[2], win.shape[3]
    factor = jax.ShapeDtypeStruct((NUM_MODULES, amino * width, seqs), BF16)
    outs = [
        factor,
        factor,
        jax.ShapeDtypeStruct((NUM_MODULES, 2, feats, seqs), F32),
        jax.ShapeDtypeStruct((NUM_MODULES, 2, hidden, feats), BF16),
    ]
    outs += [jax.ShapeDtypeStruct(x.shape, x.dtype) for x in load[3:]]
    load = [pltpu.with_memory_space_constraint(x, pltpu.HBM) for x in load]
    got = pl.pallas_call(
        functools.partial(own_kernel, seqs, amino, n_first, len(load)),
        out_shape=outs,
        in_specs=[pl.BlockSpec(memory_space=pltpu.HBM)] * len(load),
        out_specs=[pl.BlockSpec(memory_space=pltpu.VMEM)] * len(outs),
        scratch_shapes=[pltpu.VMEM(x.shape, x.dtype) for x in load[:3]]
        + [
            pltpu.VMEM((feats, amino * seqs), F32),
            pltpu.VMEM((amino * width, seqs), F32),
            pltpu.SemaphoreType.DMA((len(load),)),
        ],
        compiler_params=pltpu.CompilerParams(vmem_limit_bytes=VMEM_LIMIT),
        cost_estimate=pl.CostEstimate(flops=4_000_000_000, bytes_accessed=500_000, transcendentals=0),
        name="own",
    )(*load)
    return list(got[:4]), list(got[4:])


def far_kernel(seqs, amino, m_ref, gains, w_in, w_out, w_r, right_out, state):
    for step in range(NUM_MODULES):
        source = state if step else m_ref
        target = None if step == NUM_MODULES - 1 else state
        msa_module(
            step, seqs, amino, source, gains, w_in, w_out, None, w_r, target, None, right_out.at[step], None
        )


def far_call(seqs, amino, m, gains, w_in, w_out, w_r):
    return pl.pallas_call(
        functools.partial(far_kernel, seqs, amino),
        out_shape=jax.ShapeDtypeStruct((NUM_MODULES, amino * w_r.shape[1], seqs), BF16),
        in_specs=[pl.BlockSpec(memory_space=pltpu.VMEM)] * 5,
        out_specs=pl.BlockSpec(memory_space=pltpu.VMEM),
        scratch_shapes=[pltpu.VMEM((w_in.shape[3], amino * seqs), F32)],
        compiler_params=pltpu.CompilerParams(vmem_limit_bytes=VMEM_LIMIT),
        cost_estimate=pl.CostEstimate(flops=3_000_000_000, bytes_accessed=500_000, transcendentals=0),
        name="far",
    )(m, gains, w_in, w_out, w_r)


def swap_groups(parts, width):
    n = len(parts)
    lanes = parts[0].shape[1]
    group = lax.broadcasted_iota(jnp.int32, parts[0].shape, 1) // width
    bit = 1
    while bit < n:
        low = (group & bit) == 0
        shift = bit * width
        new = list(parts)
        for a in range(n):
            if a & bit == 0:
                x, y = parts[a], parts[a | bit]
                new[a] = jnp.where(low, x, pltpu.roll(y, shift, 1))
                new[a | bit] = jnp.where(low, pltpu.roll(x, lanes - shift, 1), y)
        parts = new
        bit *= 2
    return parts


def pair_kernel(first, n_raw, n_col, n_dep, amino, width, depth, n_left, starts, *refs):
    raw, refs = refs[:n_raw], refs[n_raw:]
    lefts, refs = refs[:n_left], refs[n_left:]
    rights, refs = refs[: len(starts)], refs[len(starts) :]
    w_ref, b_ref, keep_ref, send_ref = refs[:4]
    n_right = len(starts)
    per_dep = n_col // n_dep
    pair_ch = w_ref.shape[2]
    groups = LANES // width
    both = 2 * amino
    tiles = amino * width // LANES
    rows_tile = groups * amino
    if first:
        left, ls = refs[4:]
        seqs = ls.shape[3]
        col, dep = lax.axis_index("col"), lax.axis_index("dep")
        for dc in range(n_col):
            source = lax.rem(col - dc + n_col, n_col)
            slot = lax.rem(source - dep * per_dep + n_col, n_col)
            for step in range(NUM_MODULES):
                ls[slot, step] = lefts[dc][step].astype(F32)
        for step in range(NUM_MODULES):
            for u in range(per_dep):
                rows = jnp.concatenate(
                    [ls[u, step].reshape(width, amino, seqs), ls[per_dep + u, step].reshape(width, amino, seqs)],
                    axis=1,
                )
                left[step, u] = rows.reshape(width * both, seqs).astype(BF16)
    else:
        (left,) = lefts
    if raw:
        right, state = refs[4:]
        far_kernel(left.shape[3], amino, *raw, right.at[0], state)
        rights, starts = [right], (0,)
        n_right = 1

    def swapped(outer):
        bigs = []
        for big in range(width // groups):
            first = big * groups
            bigs.append(
                swap_groups([outer[(first + k) * both : (first + k + 1) * both] for k in range(groups)], width)
            )
        return jnp.concatenate([jnp.concatenate([x[k] for x in bigs], axis=1) for k in range(groups)], axis=0)

    items = [
        (step, u, k, t)
        for step in range(NUM_MODULES)
        for u in range(per_dep)
        for k in range(n_right)
        for t in range(tiles)
    ]

    def multiply(step, u, k, t):
        tile = rights[k][starts[k], step, t * LANES : (t + 1) * LANES, :]
        return dot_nt(left[step, u], tile).astype(BF16)

    def finish(step, u, k, t, lhs):
        got = (dot_nn(lhs, w_ref[step]) * (1.0 / depth)).reshape(groups, both, pair_ch)
        rows = slice(t * rows_tile, (t + 1) * rows_tile)
        keep_ref[step, u, k, rows, :] = got[:, :amino].reshape(rows_tile, pair_ch) + b_ref[step : step + 1, :]
        send_ref[step, u, k, rows, :] = got[:, amino:].reshape(rows_tile, pair_ch)

    outer, lhs = multiply(*items[0]), None
    for n in range(len(items) + 1):
        after = multiply(*items[n + 1]) if n + 1 < len(items) else None
        if n >= 1:
            finish(*items[n - 1], lhs)
        if n < len(items):
            lhs = swapped(outer)
        outer = after


def pair_call(name, n_col, n_dep, amino, width, depth, lefts, rights, w, b, raw=()):
    first = len(lefts) > 1
    pair_ch = w.shape[2]
    per_dep = n_col // n_dep
    factors, starts = zip(*rights) if rights else ((), ())
    seqs = lefts[0].shape[-1]
    n_right = max(len(rights), 1)
    out = jax.ShapeDtypeStruct((NUM_MODULES, per_dep, n_right, amino * amino, pair_ch), F32)
    outs, scratch = [out, out], []
    if raw:
        scratch += [
            pltpu.VMEM((1, NUM_MODULES, amino * width, seqs), BF16),
            pltpu.VMEM((raw[2].shape[3], amino * seqs), F32),
        ]
    if first:
        outs.append(jax.ShapeDtypeStruct((NUM_MODULES, per_dep, 2 * amino * width, seqs), BF16))
        scratch.append(pltpu.VMEM((n_col, NUM_MODULES, amino * width, seqs), F32))
    return pl.pallas_call(
        functools.partial(pair_kernel, first, len(raw), n_col, n_dep, amino, width, depth, len(lefts), starts),
        out_shape=outs,
        in_specs=[pl.BlockSpec(memory_space=pltpu.VMEM)] * (len(raw) + len(lefts) + len(factors) + 2),
        out_specs=[pl.BlockSpec(memory_space=pltpu.VMEM)] * len(outs),
        scratch_shapes=scratch,
        compiler_params=pltpu.CompilerParams(vmem_limit_bytes=VMEM_LIMIT),
        cost_estimate=pl.CostEstimate(
            flops=1_000_000, bytes_accessed=1000, transcendentals=0
        ),
        name="pair" + name,
    )(*raw, *lefts, *factors, w, b)


def trans_kernel(last, n_row, n_col, amino, cols, steps, next_steps, *refs):
    parts, refs = refs[: 2 * len(steps)], refs[2 * len(steps) :]
    if last:
        start_ref, done_ref, g_ref, win_ref, wout_ref, out_ref = refs
    else:
        next_ref, z_ref, g_ref, win_ref, wout_ref, out_ref, after_ref = refs
    ratio = n_row // n_col
    row, col = lax.axis_index("row"), lax.axis_index("col")
    per_dep = parts[0].shape[1]

    def places(steps):
        found = []
        for u in range(per_dep):
            for dr, dc in steps:
                off = lax.rem(lax.rem(row, ratio) - dr + ratio, ratio)
                first = (off * n_col + lax.rem(col - dc + n_col, n_col)) * amino
                found += [u * amino * cols + first + j for j in range(amino)]
        return found

    def gather(steps):
        return jnp.concatenate([z_ref[pl.ds(at, amino, stride=cols), :] for at in places(steps)], axis=0)

    def blocks(step, refs):
        return jnp.concatenate(
            [
                functools.reduce(jnp.add, [ref[step, u, i] for ref in group])
                for u in range(per_dep)
                for group in refs
                for i in range(group[0].shape[2])
            ],
            axis=0,
        )

    flat = [step for group in steps for step in group]
    if last:
        z = start_ref[...]
        out_ref[...] = done_ref[...]
    else:
        z = gather(flat)
        after_ref[...] = gather(next_steps) + blocks(0, [(next_ref,)])
    for step in range(NUM_MODULES):
        pairs = [(parts[2 * k], parts[2 * k + 1]) for k in range(len(steps))]
        if last and step == 0:
            pairs = [x[1:] for x in pairs]
        z = z + blocks(step, pairs)
        xp = norm_lanes(z, g_ref[step : step + 1, :]).astype(BF16)
        wide = dot_nn(xp, jnp.concatenate([win_ref[step, 0], win_ref[step, 1]], axis=1))
        half = wide.shape[1] // 2
        hidden = (silu_of_double(wide[:, :half] * 0.5) * wide[:, half:]).astype(BF16)
        z = z + dot_nn(hidden, wout_ref[step])
    for k, at in enumerate(places(flat)):
        out_ref[pl.ds(at, amino, stride=cols), :] = z[k * amino : (k + 1) * amino, :]


def trans_call(name, last, n_row, n_col, amino, cols, steps, parts, next_steps, ins, g, win, wout):
    per_dep, pair_ch = parts[0].shape[1], g.shape[1]
    outs = [jax.ShapeDtypeStruct((per_dep * amino * cols, pair_ch), F32)]
    if not last:
        outs.append(jax.ShapeDtypeStruct((per_dep * len(next_steps) * amino * amino, pair_ch), F32))
    return pl.pallas_call(
        functools.partial(trans_kernel, last, n_row, n_col, amino, cols, steps, next_steps),
        out_shape=outs,
        in_specs=[pl.BlockSpec(memory_space=pltpu.VMEM)] * (len(parts) + len(ins) + 3),
        out_specs=[pl.BlockSpec(memory_space=pltpu.VMEM)] * len(outs),
        compiler_params=pltpu.CompilerParams(vmem_limit_bytes=VMEM_LIMIT),
        cost_estimate=pl.CostEstimate(flops=1_400_000_000, bytes_accessed=1_500_000, transcendentals=0),
        name="trans" + name,
    )(*parts, *ins, g, win, wout)


def per_device(n_row, n_col, n_dep, msa, pair, g_ff, w_in, w_out, g_op, w_l, w_r, w_res, b_res, g_pair, p_in, p_out):
    seqs, amino, feats = msa.shape
    width = w_l.shape[2]
    depth = seqs * n_dep
    ratio = n_row // n_col
    cols = amino * n_row
    row, col = lax.axis_index("row"), lax.axis_index("col")

    def rows_by(k):
        return lambda x: lax.ppermute(x, "row", [(r, (r + k) % n_row) for r in range(n_row)])

    def group_by(k):
        pairs = [(r, r // ratio * ratio + (r % ratio + k) % ratio) for r in range(n_row)]
        return lambda x: lax.ppermute(x, "row", pairs)

    def cols_by(k):
        return lambda x: lax.ppermute(x, "col", [(c, (c + k) % n_col) for c in range(n_col)])

    def pick(items, index):
        got = items[0]
        for k in range(1, len(items)):
            got = jnp.where(index == k, items[k], got)
        return got

    def spread_far(right):
        return [right] + [rows_by(k * ratio)(right) for k in range(1, n_col)]

    def moved(x, dr, dc):
        pairs = []
        for r in range(n_row):
            to = r // ratio * ratio + (r % ratio + dr) % ratio
            pairs += [(r * n_col + c, to * n_col + (c + dc) % n_col) for c in range(n_col)]
        return lax.ppermute(x, ("row", "col"), pairs)

    def spread(items):
        group = row // ratio
        wanted = [pick(items, (group - (col + dc) + 2 * n_col) % n_col) for dc in range(n_col)]
        return lambda dr, dc: moved(wanted[dc], dr, dc) if dr or dc else wanted[0]

    w_out, w_l, w_r = (w.transpose(0, 2, 1) for w in (w_out, w_l, w_r))
    m = msa.transpose(1, 2, 0)
    z = pair.reshape(-1, pair.shape[2])
    far = [rows_by(k * ratio)(m) for k in range(1, n_col)]
    load = [g_ff, w_in, g_op, m, w_out, w_l, w_r, w_res, b_res, g_pair, p_in, p_out, z]
    (left, right, gains, w_in), load = own_call(seqs, amino, load, 7)
    m, w_out, w_l, w_r, w_res, b_res, g_pair, p_in, p_out, z = load
    lefts = [left] + [cols_by(dc)(left) for dc in range(1, n_col)]
    others = [(dr, dc) for dr in range(ratio) for dc in range(n_col) if dr or dc]
    others.sort(key=lambda step: (min(step[0], ratio - step[0]) + min(step[1], n_col - step[1])), reverse=True)
    tools = (gains, w_in, w_out, w_r)
    first = (spread([m] + far)(*others[0]), *tools)
    take = spread([right] + [far_call(seqs, amino, x, *tools) for x in far])
    per = len(others) - 1 if ratio * n_col <= 4 else n_col
    steps = [[(0, 0)], others[:1]] + [others[k : k + per] for k in range(1, len(others), per)]
    parts = []
    for k, group in enumerate(steps):
        raw = first if k == 1 else ()
        rights = [] if raw else [(take(*step)[None], 0) for step in group]
        if k > 1:
            lefts, parts[-2] = lax.optimization_barrier((lefts, parts[-2]))
        keep, send, *lead = pair_call(str(k), n_col, n_dep, amino, width, depth, lefts, rights, w_res, b_res, raw)
        lefts = lead or lefts
        parts += [keep, lax.ppermute(send, "dep", [(d, (d + 1) % n_dep) for d in range(n_dep)])]
    call = lambda name, last, *args: trans_call(
        name, last, n_row, n_col, amino, cols, *args, g_pair, p_in, p_out
    )
    most, start = call("0", False, steps[:-1], parts[:-2], steps[-1], [parts[-2], z])
    (z,) = call("1", True, steps[-1:], parts[-2:], [], [start, most])
    return z.reshape(pair.shape)


def solution(mesh):
    return jax.shard_map(
        functools.partial(per_device, mesh.shape["row"], mesh.shape["col"], mesh.shape["dep"]),
        mesh=mesh,
        in_specs=(
            P(("grp", "dep"), ("row", "col"), None),
            P(("grp", "row", "dep"), "col", None),
        )
        + (P(),) * 11,
        out_specs=P(("grp", "row", "dep"), "col", None),
        check_vma=False,
    )
```

```python
import functools

import jax
import jax.numpy as jnp
from jax import lax
from jax.experimental import pallas as pl
from jax.experimental.pallas import tpu as pltpu
from jax.sharding import PartitionSpec as P

NUM_MODULES = 2
LANES = 128
SUB = 8
F32 = jnp.float32
BF16 = jnp.bfloat16
VMEM_LIMIT = 32 * 1024 * 1024


def dot_tn(a, b):
    return lax.dot_general(a, b, (((0,), (0,)), ((), ())), preferred_element_type=F32)


def dot_nt(a, b):
    return lax.dot_general(a, b, (((1,), (1,)), ((), ())), preferred_element_type=F32)


def dot_nn(a, b):
    return lax.dot_general(a, b, (((1,), (0,)), ((), ())), preferred_element_type=F32)


def silu_of_double(x):
    return x * jnp.tanh(x) + x


def norm_rows(m, gain):
    mean = jnp.mean(m, axis=0, keepdims=True)
    centered = m - mean
    var = jnp.mean(centered * centered, axis=0, keepdims=True)
    return centered * lax.rsqrt(var + 1e-05) * gain


def norm_lanes(x, gain):
    mean = jnp.mean(x, axis=1, keepdims=True)
    centered = x - mean
    var = jnp.mean(centered * centered, axis=1, keepdims=True)
    return centered * lax.rsqrt(var + 1e-05) * gain


def msa_module(step, seqs, amino, m_ref, gains, w_in, w_out, w_l, w_r, m_out, left_out, right_out, ls):
    width = w_r.shape[1]
    per = 8
    lanes = per * seqs
    three = len(m_ref.shape) == 3
    gain1 = jnp.concatenate([gains[step, 0]] * per, axis=1)
    gain2 = jnp.concatenate([gains[step, 1]] * per, axis=1)
    for start in range(0, amino, per):
        here = slice(start * seqs, start * seqs + lanes)
        if three:
            m = jnp.concatenate([m_ref[start + k] for k in range(per)], axis=1).astype(F32)
        else:
            m = m_ref[:, here]
        xm = norm_rows(m, gain1).astype(BF16)
        gate = dot_nn(w_in[step, 0], xm)
        upper = dot_nn(w_in[step, 1], xm)
        hidden = (silu_of_double(gate) * upper).astype(BF16)
        m = m + dot_nn(w_out[step], hidden)
        if m_out is not None:
            m_out[:, here] = m
        xo = norm_rows(m, gain2).astype(BF16)
        right = dot_nn(w_r[step], xo)
        if left_out is not None:
            left = dot_nn(w_l[step], xo)
        for k in range(per):
            rows = slice((start + k) * width, (start + k + 1) * width)
            right_out[rows, :] = right[:, k * seqs : (k + 1) * seqs].astype(BF16)
            if left_out is not None:
                ls[rows, :] = left[:, k * seqs : (k + 1) * seqs]
    if left_out is not None:
        for p in range(0, width, 2):
            pair = [ls[pl.ds(p + k, amino, stride=width), :] for k in range(2)]
            left_out[p * amino : (p + 2) * amino, :] = jnp.concatenate(pair, axis=0).astype(BF16)


def own_kernel(seqs, amino, n_first, n_load, *refs):
    srcs, refs = refs[:n_load], refs[n_load:]
    (lefts_out, rights_out, gains, w_in), refs = refs[:4], refs[4:]
    dsts, (g1_ref, win_ref, g2_ref, state, ls, sems) = refs[: n_load - 3], refs[n_load - 3 :]
    dsts = (g1_ref, win_ref, g2_ref) + tuple(dsts)
    copies = [pltpu.make_async_copy(s, d, sems.at[k]) for k, (s, d) in enumerate(zip(srcs, dsts))]
    for copy in copies:
        copy.start()
    for copy in copies[:n_first]:
        copy.wait()
    m_ref, w_out, w_l, w_r = dsts[3:7]
    for step in range(NUM_MODULES):
        for k, g_ref in enumerate((g1_ref, g2_ref)):
            row = g_ref[step : step + 1, :]
            gains[step, k] = jnp.broadcast_to(row, (seqs, row.shape[1])).T
        for k in range(2):
            w_in[step, k] = win_ref[step, k].T * (1.0 if k else 0.5)
    for step in range(NUM_MODULES):
        source = state if step else m_ref
        target = None if step == NUM_MODULES - 1 else state
        msa_module(
            step, seqs, amino, source, gains, w_in, w_out, w_l, w_r, target, lefts_out.at[step], rights_out.at[step], ls
        )
    for copy in copies[n_first:]:
        copy.wait()


def own_call(seqs, amino, load, n_first):
    g1, win, g2, m, w_out, w_l, w_r = load[:7]
    width, feats, hidden = w_l.shape[1], win.shape[2], win.shape[3]
    factor = jax.ShapeDtypeStruct((NUM_MODULES, amino * width, seqs), BF16)
    outs = [
        factor,
        factor,
        jax.ShapeDtypeStruct((NUM_MODULES, 2, feats, seqs), F32),
        jax.ShapeDtypeStruct((NUM_MODULES, 2, hidden, feats), BF16),
    ]
    outs += [jax.ShapeDtypeStruct(x.shape, x.dtype) for x in load[3:]]
    load = [pltpu.with_memory_space_constraint(x, pltpu.HBM) for x in load]
    got = pl.pallas_call(
        functools.partial(own_kernel, seqs, amino, n_first, len(load)),
        out_shape=outs,
        in_specs=[pl.BlockSpec(memory_space=pltpu.HBM)] * len(load),
        out_specs=[pl.BlockSpec(memory_space=pltpu.VMEM)] * len(outs),
        scratch_shapes=[pltpu.VMEM(x.shape, x.dtype) for x in load[:3]]
        + [
            pltpu.VMEM((feats, amino * seqs), F32),
            pltpu.VMEM((amino * width, seqs), F32),
            pltpu.SemaphoreType.DMA((len(load),)),
        ],
        compiler_params=pltpu.CompilerParams(vmem_limit_bytes=VMEM_LIMIT),
        cost_estimate=pl.CostEstimate(flops=4_000_000_000, bytes_accessed=500_000, transcendentals=0),
        name="own",
    )(*load)
    return list(got[:4]), list(got[4:])


def far_kernel(seqs, amino, m_ref, gains, w_in, w_out, w_r, right_out, state):
    for step in range(NUM_MODULES):
        source = state if step else m_ref
        target = None if step == NUM_MODULES - 1 else state
        msa_module(
            step, seqs, amino, source, gains, w_in, w_out, None, w_r, target, None, right_out.at[step], None
        )


def far_call(seqs, amino, m, gains, w_in, w_out, w_r):
    return pl.pallas_call(
        functools.partial(far_kernel, seqs, amino),
        out_shape=jax.ShapeDtypeStruct((NUM_MODULES, amino * w_r.shape[1], seqs), BF16),
        in_specs=[pl.BlockSpec(memory_space=pltpu.VMEM)] * 5,
        out_specs=pl.BlockSpec(memory_space=pltpu.VMEM),
        scratch_shapes=[pltpu.VMEM((w_in.shape[3], amino * seqs), F32)],
        compiler_params=pltpu.CompilerParams(vmem_limit_bytes=VMEM_LIMIT),
        cost_estimate=pl.CostEstimate(flops=1_000_000, bytes_accessed=500_000, transcendentals=0),
        name="far",
    )(m, gains, w_in, w_out, w_r)


def swap_groups(parts, width):
    n = len(parts)
    lanes = parts[0].shape[1]
    group = lax.broadcasted_iota(jnp.int32, parts[0].shape, 1) // width
    bit = 1
    while bit < n:
        low = (group & bit) == 0
        shift = bit * width
        new = list(parts)
        for a in range(n):
            if a & bit == 0:
                x, y = parts[a], parts[a | bit]
                new[a] = jnp.where(low, x, pltpu.roll(y, shift, 1))
                new[a | bit] = jnp.where(low, pltpu.roll(x, lanes - shift, 1), y)
        parts = new
        bit *= 2
    return parts


def pair_kernel(first, n_raw, n_col, n_dep, amino, width, depth, n_left, starts, *refs):
    raw, refs = refs[:n_raw], refs[n_raw:]
    lefts, refs = refs[:n_left], refs[n_left:]
    rights, refs = refs[: len(starts)], refs[len(starts) :]
    w_ref, b_ref, keep_ref, send_ref = refs[:4]
    n_right = len(starts)
    per_dep = n_col // n_dep
    pair_ch = w_ref.shape[2]
    groups = LANES // width
    both = 2 * amino
    tiles = amino * width // LANES
    rows_tile = groups * amino
    if first:
        left, ls = refs[4:]
        seqs = ls.shape[3]
        col, dep = lax.axis_index("col"), lax.axis_index("dep")
        for dc in range(n_col):
            source = lax.rem(col - dc + n_col, n_col)
            slot = lax.rem(source - dep * per_dep + n_col, n_col)
            for step in range(NUM_MODULES):
                ls[slot, step] = lefts[dc][step].astype(F32)
        for step in range(NUM_MODULES):
            for u in range(per_dep):
                rows = jnp.concatenate(
                    [ls[u, step].reshape(width, amino, seqs), ls[per_dep + u, step].reshape(width, amino, seqs)],
                    axis=1,
                )
                left[step, u] = rows.reshape(width * both, seqs).astype(BF16)
    else:
        (left,) = lefts
    if raw:
        right, state = refs[4:]
        far_kernel(left.shape[3], amino, *raw, right.at[0], state)
        rights, starts = [right], (0,)
        n_right = 1

    def swapped(outer):
        bigs = []
        for big in range(width // groups):
            first = big * groups
            bigs.append(
                swap_groups([outer[(first + k) * both : (first + k + 1) * both] for k in range(groups)], width)
            )
        return jnp.concatenate([jnp.concatenate([x[k] for x in bigs], axis=1) for k in range(groups)], axis=0)

    items = [
        (step, u, k, t)
        for step in range(NUM_MODULES)
        for u in range(per_dep)
        for k in range(n_right)
        for t in range(tiles)
    ]

    def multiply(step, u, k, t):
        tile = rights[k][starts[k], step, t * LANES : (t + 1) * LANES, :]
        return dot_nt(left[step, u], tile).astype(BF16)

    def finish(step, u, k, t, lhs):
        got = (dot_nn(lhs, w_ref[step]) * (1.0 / depth)).reshape(groups, both, pair_ch)
        rows = slice(t * rows_tile, (t + 1) * rows_tile)
        keep_ref[step, u, k, rows, :] = got[:, :amino].reshape(rows_tile, pair_ch) + b_ref[step : step + 1, :]
        send_ref[step, u, k, rows, :] = got[:, amino:].reshape(rows_tile, pair_ch)

    outer, lhs = multiply(*items[0]), None
    for n in range(len(items) + 1):
        after = multiply(*items[n + 1]) if n + 1 < len(items) else None
        if n >= 1:
            finish(*items[n - 1], lhs)
        if n < len(items):
            lhs = swapped(outer)
        outer = after


def pair_call(name, n_col, n_dep, amino, width, depth, lefts, rights, w, b, raw=()):
    first = len(lefts) > 1
    pair_ch = w.shape[2]
    per_dep = n_col // n_dep
    factors, starts = zip(*rights) if rights else ((), ())
    seqs = lefts[0].shape[-1]
    n_right = max(len(rights), 1)
    out = jax.ShapeDtypeStruct((NUM_MODULES, per_dep, n_right, amino * amino, pair_ch), F32)
    outs, scratch = [out, out], []
    if raw:
        scratch += [
            pltpu.VMEM((1, NUM_MODULES, amino * width, seqs), BF16),
            pltpu.VMEM((raw[2].shape[3], amino * seqs), F32),
        ]
    if first:
        outs.append(jax.ShapeDtypeStruct((NUM_MODULES, per_dep, 2 * amino * width, seqs), BF16))
        scratch.append(pltpu.VMEM((n_col, NUM_MODULES, amino * width, seqs), F32))
    return pl.pallas_call(
        functools.partial(pair_kernel, first, len(raw), n_col, n_dep, amino, width, depth, len(lefts), starts),
        out_shape=outs,
        in_specs=[pl.BlockSpec(memory_space=pltpu.VMEM)] * (len(raw) + len(lefts) + len(factors) + 2),
        out_specs=[pl.BlockSpec(memory_space=pltpu.VMEM)] * len(outs),
        scratch_shapes=scratch,
        compiler_params=pltpu.CompilerParams(vmem_limit_bytes=VMEM_LIMIT),
        cost_estimate=pl.CostEstimate(
            flops=1_000_000, bytes_accessed=1000, transcendentals=0
        ),
        name="pair" + name,
    )(*raw, *lefts, *factors, w, b)


def trans_kernel(last, n_row, n_col, amino, cols, steps, next_steps, *refs):
    parts, refs = refs[: 2 * len(steps)], refs[2 * len(steps) :]
    if last:
        start_ref, done_ref, g_ref, win_ref, wout_ref, out_ref = refs
    else:
        next_ref, z_ref, g_ref, win_ref, wout_ref, out_ref, after_ref = refs
    ratio = n_row // n_col
    row, col = lax.axis_index("row"), lax.axis_index("col")
    per_dep = parts[0].shape[1]

    def places(steps):
        found = []
        for u in range(per_dep):
            for dr, dc in steps:
                off = lax.rem(lax.rem(row, ratio) - dr + ratio, ratio)
                first = (off * n_col + lax.rem(col - dc + n_col, n_col)) * amino
                found += [u * amino * cols + first + j for j in range(amino)]
        return found

    def gather(steps):
        return jnp.concatenate([z_ref[pl.ds(at, amino, stride=cols), :] for at in places(steps)], axis=0)

    def blocks(step, refs):
        return jnp.concatenate(
            [
                functools.reduce(jnp.add, [ref[step, u, i] for ref in group])
                for u in range(per_dep)
                for group in refs
                for i in range(group[0].shape[2])
            ],
            axis=0,
        )

    flat = [step for group in steps for step in group]
    if last:
        z = start_ref[...]
        out_ref[...] = done_ref[...]
    else:
        z = gather(flat)
        after_ref[...] = gather(next_steps) + blocks(0, [(next_ref,)])
    for step in range(NUM_MODULES):
        pairs = [(parts[2 * k], parts[2 * k + 1]) for k in range(len(steps))]
        if last and step == 0:
            pairs = [x[1:] for x in pairs]
        z = z + blocks(step, pairs)
        xp = norm_lanes(z, g_ref[step : step + 1, :]).astype(BF16)
        gate = dot_nn(xp, win_ref[step, 0]) * 0.5
        upper = dot_nn(xp, win_ref[step, 1])
        hidden = (silu_of_double(gate) * upper).astype(BF16)
        z = z + dot_nn(hidden, wout_ref[step])
    for k, at in enumerate(places(flat)):
        out_ref[pl.ds(at, amino, stride=cols), :] = z[k * amino : (k + 1) * amino, :]


def trans_call(name, last, n_row, n_col, amino, cols, steps, parts, next_steps, ins, g, win, wout):
    per_dep, pair_ch = parts[0].shape[1], g.shape[1]
    outs = [jax.ShapeDtypeStruct((per_dep * amino * cols, pair_ch), F32)]
    if not last:
        outs.append(jax.ShapeDtypeStruct((per_dep * len(next_steps) * amino * amino, pair_ch), F32))
    return pl.pallas_call(
        functools.partial(trans_kernel, last, n_row, n_col, amino, cols, steps, next_steps),
        out_shape=outs,
        in_specs=[pl.BlockSpec(memory_space=pltpu.VMEM)] * (len(parts) + len(ins) + 3),
        out_specs=[pl.BlockSpec(memory_space=pltpu.VMEM)] * len(outs),
        compiler_params=pltpu.CompilerParams(vmem_limit_bytes=VMEM_LIMIT),
        cost_estimate=pl.CostEstimate(flops=1_400_000_000, bytes_accessed=1_500_000, transcendentals=0),
        name="trans" + name,
    )(*parts, *ins, g, win, wout)


def per_device(n_row, n_col, n_dep, msa, pair, g_ff, w_in, w_out, g_op, w_l, w_r, w_res, b_res, g_pair, p_in, p_out):
    seqs, amino, feats = msa.shape
    width = w_l.shape[2]
    depth = seqs * n_dep
    ratio = n_row // n_col
    cols = amino * n_row
    row, col = lax.axis_index("row"), lax.axis_index("col")

    def rows_by(k):
        return lambda x: lax.ppermute(x, "row", [(r, (r + k) % n_row) for r in range(n_row)])

    def group_by(k):
        pairs = [(r, r // ratio * ratio + (r % ratio + k) % ratio) for r in range(n_row)]
        return lambda x: lax.ppermute(x, "row", pairs)

    def cols_by(k):
        return lambda x: lax.ppermute(x, "col", [(c, (c + k) % n_col) for c in range(n_col)])

    def pick(items, index):
        got = items[0]
        for k in range(1, len(items)):
            got = jnp.where(index == k, items[k], got)
        return got

    def spread_far(right):
        return [right] + [rows_by(k * ratio)(right) for k in range(1, n_col)]

    def moved(x, dr, dc):
        pairs = []
        for r in range(n_row):
            to = r // ratio * ratio + (r % ratio + dr) % ratio
            pairs += [(r * n_col + c, to * n_col + (c + dc) % n_col) for c in range(n_col)]
        return lax.ppermute(x, ("row", "col"), pairs)

    def spread(items):
        group = row // ratio
        wanted = [pick(items, (group - (col + dc) + 2 * n_col) % n_col) for dc in range(n_col)]
        return lambda dr, dc: moved(wanted[dc], dr, dc) if dr or dc else wanted[0]

    w_out, w_l, w_r = (w.transpose(0, 2, 1) for w in (w_out, w_l, w_r))
    m = msa.transpose(1, 2, 0)
    z = pair.reshape(-1, pair.shape[2])
    far = [rows_by(k * ratio)(m) for k in range(1, n_col)]
    load = [g_ff, w_in, g_op, m, w_out, w_l, w_r, w_res, b_res, g_pair, p_in, p_out, z]
    (left, right, gains, w_in), load = own_call(seqs, amino, load, 7)
    m, w_out, w_l, w_r, w_res, b_res, g_pair, p_in, p_out, z = load
    lefts = [left] + [cols_by(dc)(left) for dc in range(1, n_col)]
    others = [(dr, dc) for dr in range(ratio) for dc in range(n_col) if dr or dc]
    others.sort(key=lambda step: (min(step[0], ratio - step[0]) + min(step[1], n_col - step[1])), reverse=True)
    tools = (gains, w_in, w_out, w_r)
    first = (spread([m] + far)(*others[0]), *tools)
    take = spread([right] + [far_call(seqs, amino, x, *tools) for x in far])
    per = len(others) - 1 if ratio * n_col <= 4 else n_col
    steps = [[(0, 0)], others[:1]] + [others[k : k + per] for k in range(1, len(others), per)]
    parts = []
    for k, group in enumerate(steps):
        raw = first if k == 1 else ()
        rights = [] if raw else [(take(*step)[None], 0) for step in group]
        if k > 1:
            lefts, parts[-2] = lax.optimization_barrier((lefts, parts[-2]))
        keep, send, *lead = pair_call(str(k), n_col, n_dep, amino, width, depth, lefts, rights, w_res, b_res, raw)
        lefts = lead or lefts
        parts += [keep, lax.ppermute(send, "dep", [(d, (d + 1) % n_dep) for d in range(n_dep)])]
    call = lambda name, last, *args: trans_call(
        name, last, n_row, n_col, amino, cols, *args, g_pair, p_in, p_out
    )
    most, start = call("0", False, steps[:-1], parts[:-2], steps[-1], [parts[-2], z])
    (z,) = call("1", True, steps[-1:], parts[-2:], [], [start, most])
    return z.reshape(pair.shape)


def solution(mesh):
    return jax.shard_map(
        functools.partial(per_device, mesh.shape["row"], mesh.shape["col"], mesh.shape["dep"]),
        mesh=mesh,
        in_specs=(
            P(("grp", "dep"), ("row", "col"), None),
            P(("grp", "row", "dep"), "col", None),
        )
        + (P(),) * 11,
        out_specs=P(("grp", "row", "dep"), "col", None),
        check_vma=False,
    )
```
